32 devices in a mesh: client: 16 (over z, y, x), param: 2 (over core).
Axes of the slice: x: 2, y: 2, z: 4, core: 2. Of those that a mesh axis runs over, the one named last changes fastest.
Arguments:
- updates: float32 [32, 128, 3584], P('client', None, 'param'), as said below
- sample_counts: int32 [32], P('client'), may hold values from 16 to 1023
Outputs:
- median: float32 [128, 3584], P('client', 'param')
- shares: float32 [32], P('client')
The draws below stay inside these ranges and needn't reach their ends.
Inputs may be any that keep to these rules, and one draw needn't show every extreme that they name: `updates`: each client's update is real-valued with every entry nonzero in general.
All inputs are finite; a program needn't handle non-finite values.
Results may differ from the reference program's by a relative error of at most 0.0001.
Values sent between devices are 32-bit elements; how exact they have to be, the bound alone decides.
A program may use at most 64 MiB of HBM per device.

```python
import math
import jax
import jax.numpy as jnp
from jax import lax

COLS = 3584
ROWS = 128
ITERS = 2
CLIENTS = 32


def draw_updates(key, part):
    subkeys = jax.random.split(jax.random.fold_in(key, 7), 8)
    common = jax.random.normal(subkeys[0], (ROWS, COLS), jnp.float32)
    column_scale = jnp.exp(jax.random.uniform(subkeys[1], (COLS,), jnp.float32, 0.0, math.log(10.0))) / 3.0
    client_scale = jnp.exp(jax.random.uniform(subkeys[2], (CLIENTS, ROWS, 1), jnp.float32, math.log(0.3), math.log(3.0)))
    ranking = jax.random.permutation(subkeys[4], CLIENTS)
    outlier = (ranking < CLIENTS // 5).astype(jnp.float32)
    magnitude = 3.0 * jnp.exp(jax.random.uniform(subkeys[5], (CLIENTS,), jnp.float32, 0.0, math.log(3.0)))
    direction = jax.random.normal(subkeys[6], (ROWS, COLS), jnp.float32)
    block_start = jax.random.randint(subkeys[7], (CLIENTS,), 0, ROWS).astype(jnp.int32)
    row_index = jnp.arange(ROWS, dtype=jnp.int32)
    offset = (row_index[None, :] - block_start[:, None] + ROWS) % ROWS
    in_block = (offset < max(ROWS // 8, 1)).astype(jnp.float32)
    shifted = ((outlier * magnitude)[:, None] * in_block)[:, :, None] * direction[None]
    client_noise = jax.random.normal(subkeys[3], (CLIENTS, ROWS, COLS), jnp.float32)
    return ((common + client_scale * client_noise + shifted) * column_scale).astype(jnp.float32)


def set_ends(values, stream_key, low, top_value):
    spot = [jax.random.randint(jax.random.fold_in(stream_key, axis), (), 0, length) for axis, length in enumerate(values.shape)]
    longest = values.shape.index(max(values.shape))
    neighbour = spot[:longest] + [(spot[longest] + 1) % values.shape[longest]] + spot[longest + 1:]
    return values.at[tuple(spot)].set(low).at[tuple(neighbour)].set(top_value)


def setup_inputs(seed: int = 0) -> dict:
    streams_of = jax.random.split(jax.random.key(seed), 3)
    return {
        "updates": draw_updates(jax.random.fold_in(streams_of[2], 71), 0),
        "sample_counts": set_ends(jax.random.randint(streams_of[1], (CLIENTS,), 16, 1024), jax.random.fold_in(streams_of[1], 1), 16, 1023).astype(jnp.int32),
    }


smoothing = 1e-06

def weighted_sum(weights, updates):
    return jnp.einsum('c,crk->rk', weights, updates, precision=lax.Precision.HIGHEST)

def reference(updates, sample_counts):
    counts_f = sample_counts.astype(jnp.float32)
    median = weighted_sum(counts_f, updates) / jnp.sum(counts_f)
    weights = counts_f
    weight_sum = jnp.sum(counts_f)
    for iteration in range(ITERS):
        distance_sq = lax.map(lambda client: jnp.sum((client - median) ** 2), updates)
        weights = counts_f / jnp.sqrt(distance_sq + smoothing)
        weight_sum = jnp.sum(weights)
        median = weighted_sum(weights, updates) / weight_sum
    shares = CLIENTS * weights / weight_sum
    return (median, shares)
```

```python
import functools

import jax
import jax.numpy as jnp
from jax import lax
from jax.experimental import pallas as pl
from jax.experimental.pallas import tpu as pltpu
from jax.sharding import PartitionSpec as P

ITERS = 2
LANES = 128
SUBLANES = 8
GROUPS = 2
CHUNKS = 2

smoothing = 1e-06


def weighted_sum(weights, updates):
    return jnp.einsum("c,crk->rk", weights, updates, precision=lax.Precision.HIGHEST)


def local_plain(updates, sample_counts):
    local_clients = updates.shape[0]
    clients = local_clients * lax.axis_size("client")
    exchanged = lax.all_to_all(updates, "client", split_axis=1, concat_axis=0, tiled=True)
    counts_f = lax.all_gather(sample_counts, "client", axis=0, tiled=True).astype(jnp.float32)
    weights = counts_f
    for iteration in range(ITERS + 1):
        weight_sum = jnp.sum(weights)
        median = weighted_sum(weights, exchanged) / weight_sum
        if iteration < ITERS:
            distance_sq = jnp.sum((exchanged - median[None]) ** 2, axis=(1, 2))
            distance_sq = lax.psum(distance_sq, ("client", "param"))
            weights = counts_f / jnp.sqrt(distance_sq + smoothing)
    offset = lax.axis_index("client") * local_clients
    shares = lax.dynamic_slice_in_dim(clients * weights / weight_sum, offset, local_clients, 0)
    return (median, shares)


def kernel(groups, members, cores, chunks, u_ref, cnt_ref, med_ref, share_ref,
           held, cnt_send, cnt_held, dist_send, dist_held, dist_rows, weight, part, part_in, last, last_in,
           own_sem, u_send, u_recv, c_send, c_recv, p_send, p_recv, l_send, l_recv, d_send, d_recv):
    nc, cols = u_ref.shape[0], u_ref.shape[-1]
    clients = nc * members
    me, core = lax.axis_index("client"), lax.axis_index("param")
    j, h = lax.rem(me, members), lax.div(me, members)
    partner = lax.rem(me + members, groups * members)
    rank = core * members + j
    width = cols // chunks

    def member(o, c):
        return {"client": h * members + lax.rem(j + o, members), "param": lax.rem(core + c, cores)}

    others = [(o, c) for c in range(cores) for o in range(members) if o or c]
    barrier = pltpu.get_barrier_semaphore()
    for o, c in others:
        pl.semaphore_signal(barrier, inc=1, device_id=member(o, c), device_id_type=pl.DeviceIdType.MESH)
    if groups > 1:
        pl.semaphore_signal(barrier, inc=1, device_id={"client": partner}, device_id_type=pl.DeviceIdType.MESH)
    own = []
    for k in range(chunks):
        sl = pl.ds(k * width, width)
        own.append(pltpu.make_async_copy(u_ref.at[:, :, j, :, sl], held.at[j, :, :, :, sl], own_sem.at[k]))
        own[-1].start()
    for c in range(nc):
        row = jnp.full((1, LANES), cnt_ref[c], jnp.int32).astype(jnp.float32)
        cnt_send[c:c + 1, :] = row
        cnt_held[j, c:c + 1, :] = row
    pl.semaphore_wait(barrier, len(others) + (groups > 1))

    def count_copy(o, slot):
        return pltpu.make_async_remote_copy(
            src_ref=cnt_send, dst_ref=cnt_held.at[slot], send_sem=c_send.at[o], recv_sem=c_recv.at[o],
            device_id={"client": h * members + lax.rem(j + o, members)}, device_id_type=pl.DeviceIdType.MESH)

    def rows_copy(o, k, slot):
        to = lax.rem(j + o, members)
        sl = pl.ds(k * width, width)
        return pltpu.make_async_remote_copy(
            src_ref=u_ref.at[:, :, to, :, sl], dst_ref=held.at[slot, :, :, :, sl],
            send_sem=u_send.at[o, k], recv_sem=u_recv.at[o, k],
            device_id={"client": h * members + to}, device_id_type=pl.DeviceIdType.MESH)

    def source(o):
        return lax.rem(j + members - o, members)

    for o in range(1, members):
        count_copy(o, j).start()
    for k in range(chunks):
        for o in range(1, members):
            rows_copy(o, k, j).start()

    def part_copy(i, k):
        sl = pl.ds(k * width, width + (LANES if k == chunks - 1 else 0))
        return pltpu.make_async_remote_copy(
            src_ref=part.at[i, :, :, sl], dst_ref=part_in.at[i, :, :, sl],
            send_sem=p_send.at[i, k], recv_sem=p_recv.at[i, k],
            device_id={"client": partner}, device_id_type=pl.DeviceIdType.MESH)

    def weights_now():
        w = [jnp.broadcast_to(weight[c:c + 1, :], (SUBLANES, LANES)) for c in range(clients)]
        total = w[0]
        for x in w[1:]:
            total = total + x
        return w, total

    def tile(t):
        return pl.ds(pl.multiple_of(t * LANES, LANES), LANES)

    def sum_tile(w, r, t):
        acc = w[0] * held[0, 0, r, :, tile(t)]
        for c in range(1, clients):
            acc = acc + w[c] * held[c // nc, c % nc, r, :, tile(t)]
        return acc

    def send_part(i):
        w, total = weights_now()
        for r in range(groups):
            part[i, r, :, pl.ds(cols, LANES)] = total
        for k in range(chunks):
            if i == 0:
                own[k].wait()
                for o in range(1, members):
                    rows_copy(o, k, source(o)).wait_recv()

            def body(t, carry):
                for r in range(groups):
                    part[i, r, :, tile(t)] = sum_tile(w, r, t)
                return carry

            lax.fori_loop(k * width // LANES, (k + 1) * width // LANES, body, 0)
            if groups > 1:
                part_copy(i, k).start()

    def distances(i):
        total = part[i, 0, :, pl.ds(cols, LANES)]
        acc = tuple(jnp.zeros((SUBLANES, LANES), jnp.float32) for _ in range(clients))
        if groups > 1:
            part_copy(i, chunks - 1).wait_recv()
            total = total + part_in[i, 0, :, pl.ds(cols, LANES)]
        inverse = 1.0 / total
        for k in range(chunks):
            if groups > 1 and k < chunks - 1:
                part_copy(i, k).wait_recv()

            def body(t, acc):
                acc = list(acc)
                for r in range(groups):
                    m = part[i, r, :, tile(t)]
                    if groups > 1:
                        m = m + part_in[i, r, :, tile(t)]
                    m = m * inverse
                    for c in range(clients):
                        d = held[c // nc, c % nc, r, :, tile(t)] - m
                        acc[c] = acc[c] + d * d
                return tuple(acc)

            acc = lax.fori_loop(k * width // LANES, (k + 1) * width // LANES, body, acc)
        for c in range(clients):
            dist_rows[c:c + 1, :] = jnp.sum(acc[c], axis=0, keepdims=True)
        eye = (lax.broadcasted_iota(jnp.int32, (clients, LANES), 0)
               == lax.broadcasted_iota(jnp.int32, (clients, LANES), 1))
        column = jnp.sum(dist_rows[...], axis=1, keepdims=True)
        row = jnp.sum(jnp.where(eye, column, 0.0), axis=0, keepdims=True)
        dist_send[i] = row
        dist_held[i, rank] = row

        def copy(n, o, c, slot):
            return pltpu.make_async_remote_copy(
                src_ref=dist_send.at[i], dst_ref=dist_held.at[i, slot],
                send_sem=d_send.at[i, n], recv_sem=d_recv.at[i, n],
                device_id=member(o, c), device_id_type=pl.DeviceIdType.MESH)

        for n, (o, c) in enumerate(others):
            copy(n, o, c, rank).start()
        for n, (o, c) in enumerate(others):
            copy(n, o, c, lax.rem(core + cores - c, cores) * members + source(o)).wait_recv()
        row = dist_held[i, 0]
        for s in range(1, cores * members):
            row = row + dist_held[i, s]
        column = jnp.sum(jnp.where(eye, jnp.broadcast_to(row, eye.shape), 0.0), axis=1, keepdims=True)
        root = jnp.sqrt(jnp.broadcast_to(column, eye.shape) + smoothing)
        for c in range(clients):
            weight[c:c + 1, :] = cnt_held[c // nc, c % nc:c % nc + 1, :] / root[c:c + 1, :]
        for n, (o, c) in enumerate(others):
            copy(n, o, c, rank).wait_send()

    for o in range(1, members):
        count_copy(o, source(o)).wait_recv()
    for c in range(clients):
        weight[c:c + 1, :] = cnt_held[c // nc, c % nc:c % nc + 1, :]
    for i in range(ITERS):
        send_part(i)
        distances(i)

    w, total = weights_now()
    final = pltpu.make_async_remote_copy(
        src_ref=last, dst_ref=last_in, send_sem=l_send, recv_sem=l_recv,
        device_id={"client": partner}, device_id_type=pl.DeviceIdType.MESH)
    if groups > 1:
        last[:, pl.ds(cols, LANES)] = total

        def body(t, carry):
            last[:, tile(t)] = sum_tile(w, 1 - h, t)
            return carry

        lax.fori_loop(0, cols // LANES, body, 0)
        final.start()

    def body(t, carry):
        med_ref[:, tile(t)] = sum_tile(w, h, t)
        return carry

    lax.fori_loop(0, cols // LANES, body, 0)
    if groups > 1:
        final.wait_recv()
        total = total + last_in[:, pl.ds(cols, LANES)]
    inverse = 1.0 / total

    def body(t, carry):
        m = med_ref[:, tile(t)]
        if groups > 1:
            m = m + last_in[:, tile(t)]
        med_ref[:, tile(t)] = m * inverse
        return carry

    lax.fori_loop(0, cols // LANES, body, 0)
    for c in range(nc):
        share = (groups * clients) * weight[pl.ds(nc * j + c, 1), :] * inverse[0:1, :]
        share_ref[c] = share[0, 0]

    for o in range(1, members):
        count_copy(o, j).wait_send()
        for k in range(chunks):
            rows_copy(o, k, j).wait_send()
    if groups > 1:
        for i in range(ITERS):
            for k in range(chunks):
                part_copy(i, k).wait_send()
        final.wait_send()


def local(updates, sample_counts):
    nc, rows, cols = updates.shape
    devices, cores = lax.axis_size("client"), lax.axis_size("param")
    groups = GROUPS if devices % GROUPS == 0 and devices > GROUPS else 1
    members = devices // groups
    chunks = CHUNKS if cols % (CHUNKS * LANES) == 0 else 1
    mine = rows // devices
    if rows % devices or mine != SUBLANES or cols % LANES or members < 2 or nc * members > LANES:
        return local_plain(updates, sample_counts)
    clients = nc * members
    f32 = jnp.float32
    dma = pltpu.SemaphoreType.DMA
    wide = cols + LANES
    return pl.pallas_call(
        functools.partial(kernel, groups, members, cores, chunks),
        out_shape=(jax.ShapeDtypeStruct((mine, cols), f32), jax.ShapeDtypeStruct((nc,), f32)),
        in_specs=[pl.BlockSpec(memory_space=pl.ANY), pl.BlockSpec(memory_space=pltpu.SMEM)],
        out_specs=(pl.BlockSpec(memory_space=pltpu.VMEM), pl.BlockSpec(memory_space=pltpu.SMEM)),
        scratch_shapes=[
            pltpu.VMEM((members, nc, groups, mine, cols), f32),
            pltpu.VMEM((nc, LANES), f32),
            pltpu.VMEM((members, nc, LANES), f32),
            pltpu.VMEM((ITERS, 1, LANES), f32),
            pltpu.VMEM((ITERS, cores * members, 1, LANES), f32),
            pltpu.VMEM((clients, LANES), f32),
            pltpu.VMEM((clients, LANES), f32),
            pltpu.VMEM((ITERS, groups, mine, wide), f32),
            pltpu.VMEM((ITERS, groups, mine, wide), f32),
            pltpu.VMEM((mine, wide), f32),
            pltpu.VMEM((mine, wide), f32),
            dma((chunks,)),
            dma((members, chunks)),
            dma((members, chunks)),
            dma((members,)),
            dma((members,)),
            dma((ITERS, chunks)),
            dma((ITERS, chunks)),
            dma,
            dma,
            dma((ITERS, cores * members)),
            dma((ITERS, cores * members)),
        ],
        compiler_params=pltpu.CompilerParams(
            collective_id=0, has_side_effects=True, vmem_limit_bytes=32 * 1024 * 1024),
        cost_estimate=pl.CostEstimate(
            flops=16 * clients * groups * mine * cols, bytes_accessed=8 * nc * rows * cols, transcendentals=0),
    )(updates.reshape(nc, groups, members, mine, cols), sample_counts)


def solution(mesh):
    return jax.shard_map(
        local,
        mesh=mesh,
        in_specs=(P("client", None, "param"), P("client")),
        out_specs=(P("client", "param"), P("client")),
        check_vma=False,
    )
```

```python
import functools

import jax
import jax.numpy as jnp
from jax import lax
from jax.experimental import pallas as pl
from jax.experimental.pallas import tpu as pltpu
from jax.sharding import PartitionSpec as P

ITERS = 2
LANES = 128
SUBLANES = 8
GROUPS = 2
CHUNK_ENDS = (0.43, 0.79, 1.0)

smoothing = 1e-06


def weighted_sum(weights, updates):
    return jnp.einsum("c,crk->rk", weights, updates, precision=lax.Precision.HIGHEST)


def local_plain(updates, sample_counts):
    local_clients = updates.shape[0]
    clients = local_clients * lax.axis_size("client")
    exchanged = lax.all_to_all(updates, "client", split_axis=1, concat_axis=0, tiled=True)
    counts_f = lax.all_gather(sample_counts, "client", axis=0, tiled=True).astype(jnp.float32)
    weights = counts_f
    for iteration in range(ITERS + 1):
        weight_sum = jnp.sum(weights)
        median = weighted_sum(weights, exchanged) / weight_sum
        if iteration < ITERS:
            distance_sq = jnp.sum((exchanged - median[None]) ** 2, axis=(1, 2))
            distance_sq = lax.psum(distance_sq, ("client", "param"))
            weights = counts_f / jnp.sqrt(distance_sq + smoothing)
    offset = lax.axis_index("client") * local_clients
    shares = lax.dynamic_slice_in_dim(clients * weights / weight_sum, offset, local_clients, 0)
    return (median, shares)


def kernel(groups, members, cores, bounds, u_ref, cnt_hbm, med_ref, share_ref,
           held, cnt_ref, cnt_send, cnt_held, dist_send, dist_held, dist_rows, weight, part, part_in, last, last_in,
           in_sem, own_sem, u_send, u_recv, c_send, c_recv, p_send, p_recv, l_send, l_recv, d_send, d_recv):
    nc, cols = u_ref.shape[0], u_ref.shape[-1]
    clients = nc * members
    me, core = lax.axis_index("client"), lax.axis_index("param")
    j, h = lax.rem(me, members), lax.div(me, members)
    partner = lax.rem(me + members, groups * members)
    rank = core * members + j
    chunks = len(bounds) - 1

    def lanes(k, extra=0):
        return pl.ds(bounds[k] * LANES, (bounds[k + 1] - bounds[k]) * LANES + extra)

    def member(o, c):
        return {"client": h * members + lax.rem(j + o, members), "param": lax.rem(core + c, cores)}

    others = [(o, c) for c in range(cores) for o in range(members) if o or c]
    barrier = pltpu.get_barrier_semaphore()
    for o, c in others:
        pl.semaphore_signal(barrier, inc=1, device_id=member(o, c), device_id_type=pl.DeviceIdType.MESH)
    if groups > 1:
        pl.semaphore_signal(barrier, inc=1, device_id={"client": partner}, device_id_type=pl.DeviceIdType.MESH)
    counts_in = pltpu.make_async_copy(cnt_hbm, cnt_ref, in_sem)
    counts_in.start()
    own = []
    for k in range(chunks):
        sl = lanes(k)
        own.append(pltpu.make_async_copy(u_ref.at[:, :, j, :, sl], held.at[j, :, :, :, sl], own_sem.at[k]))
        own[-1].start()
    counts_in.wait()
    for c in range(nc):
        row = jnp.full((1, LANES), cnt_ref[c], jnp.int32).astype(jnp.float32)
        cnt_send[c:c + 1, :] = row
        cnt_held[j, c:c + 1, :] = row
    pl.semaphore_wait(barrier, len(others) + (groups > 1))

    full = members - 1
    masks = [m for low in range(1, members // 2) for m in (low, full - low)] + [full]
    bits = [1 << b for b in range(full.bit_length())]

    def peer(o):
        m, index = masks[o - 1], 0
        for b in bits:
            flip = (m // b) % 2
            if m != full:
                flip = flip + lax.rem(core, 2) * (1 - 2 * flip)
            index = index + b * lax.rem(lax.rem(lax.div(j, b), 2) + flip, 2)
        return index

    def count_copy(o, slot):
        return pltpu.make_async_remote_copy(
            src_ref=cnt_send, dst_ref=cnt_held.at[slot], send_sem=c_send.at[o], recv_sem=c_recv.at[o],
            device_id={"client": h * members + peer(o)}, device_id_type=pl.DeviceIdType.MESH)

    def rows_copy(o, k, slot):
        to = peer(o)
        sl = lanes(k)
        return pltpu.make_async_remote_copy(
            src_ref=u_ref.at[:, :, to, :, sl], dst_ref=held.at[slot, :, :, :, sl],
            send_sem=u_send.at[o, k], recv_sem=u_recv.at[o, k],
            device_id={"client": h * members + to}, device_id_type=pl.DeviceIdType.MESH)

    def source(o):
        return lax.rem(j + members - o, members)

    for o in range(1, members):
        count_copy(o, j).start()
    for k in range(chunks):
        for o in range(1, members):
            rows_copy(o, k, j).start()

    def part_copy(i, k):
        sl = lanes(k, LANES if k == chunks - 1 else 0)
        return pltpu.make_async_remote_copy(
            src_ref=part.at[i, :, :, sl], dst_ref=part_in.at[i, :, :, sl],
            send_sem=p_send.at[i, k], recv_sem=p_recv.at[i, k],
            device_id={"client": partner}, device_id_type=pl.DeviceIdType.MESH)

    def weights_now():
        w = [jnp.broadcast_to(weight[c:c + 1, :], (SUBLANES, LANES)) for c in range(clients)]
        total = w[0]
        for x in w[1:]:
            total = total + x
        return w, total

    def tile(t):
        return pl.ds(pl.multiple_of(t * LANES, LANES), LANES)

    def sum_tile(w, r, t):
        acc = w[0] * held[0, 0, r, :, tile(t)]
        for c in range(1, clients):
            acc = acc + w[c] * held[c // nc, c % nc, r, :, tile(t)]
        return acc

    def send_part(i):
        w, total = weights_now()
        for r in range(groups):
            part[i, r, :, pl.ds(cols, LANES)] = total
        for k in range(chunks):
            if i == 0:
                own[k].wait()
                for o in range(1, members):
                    rows_copy(o, k, peer(o)).wait_recv()

            def body(t, carry):
                for r in range(groups):
                    part[i, r, :, tile(t)] = sum_tile(w, r, t)
                return carry

            lax.fori_loop(bounds[k], bounds[k + 1], body, 0)
            if groups > 1:
                part_copy(i, k).start()

    def distances(i):
        total = part[i, 0, :, pl.ds(cols, LANES)]
        acc = tuple(jnp.zeros((SUBLANES, LANES), jnp.float32) for _ in range(clients))
        if groups > 1:
            part_copy(i, chunks - 1).wait_recv()
            total = total + part_in[i, 0, :, pl.ds(cols, LANES)]
        inverse = 1.0 / total
        for k in range(chunks):
            if groups > 1 and k < chunks - 1:
                part_copy(i, k).wait_recv()

            def body(t, acc):
                acc = list(acc)
                for r in range(groups):
                    m = part[i, r, :, tile(t)]
                    if groups > 1:
                        m = m + part_in[i, r, :, tile(t)]
                    m = m * inverse
                    for c in range(clients):
                        d = held[c // nc, c % nc, r, :, tile(t)] - m
                        acc[c] = acc[c] + d * d
                return tuple(acc)

            acc = lax.fori_loop(bounds[k], bounds[k + 1], body, acc)
        for c in range(clients):
            dist_rows[c:c + 1, :] = jnp.sum(acc[c], axis=0, keepdims=True)
        eye = (lax.broadcasted_iota(jnp.int32, (clients, LANES), 0)
               == lax.broadcasted_iota(jnp.int32, (clients, LANES), 1))
        column = jnp.sum(dist_rows[...], axis=1, keepdims=True)
        row = jnp.sum(jnp.where(eye, column, 0.0), axis=0, keepdims=True)
        dist_send[i] = row
        dist_held[i, rank] = row

        def copy(n, o, c, slot):
            return pltpu.make_async_remote_copy(
                src_ref=dist_send.at[i], dst_ref=dist_held.at[i, slot],
                send_sem=d_send.at[i, n], recv_sem=d_recv.at[i, n],
                device_id=member(o, c), device_id_type=pl.DeviceIdType.MESH)

        for n, (o, c) in enumerate(others):
            copy(n, o, c, rank).start()
        for n, (o, c) in enumerate(others):
            copy(n, o, c, lax.rem(core + cores - c, cores) * members + source(o)).wait_recv()
        row = dist_held[i, 0]
        for s in range(1, cores * members):
            row = row + dist_held[i, s]
        column = jnp.sum(jnp.where(eye, jnp.broadcast_to(row, eye.shape), 0.0), axis=1, keepdims=True)
        root = jnp.sqrt(jnp.broadcast_to(column, eye.shape) + smoothing)
        for c in range(clients):
            weight[c:c + 1, :] = cnt_held[c // nc, c % nc:c % nc + 1, :] / root[c:c + 1, :]
        for n, (o, c) in enumerate(others):
            copy(n, o, c, rank).wait_send()

    for o in range(1, members):
        count_copy(o, peer(o)).wait_recv()
    for c in range(clients):
        weight[c:c + 1, :] = cnt_held[c // nc, c % nc:c % nc + 1, :]
    for i in range(ITERS):
        send_part(i)
        distances(i)

    w, total = weights_now()
    final = pltpu.make_async_remote_copy(
        src_ref=last, dst_ref=last_in, send_sem=l_send, recv_sem=l_recv,
        device_id={"client": partner}, device_id_type=pl.DeviceIdType.MESH)
    if groups > 1:
        last[:, pl.ds(cols, LANES)] = total

        def body(t, carry):
            last[:, tile(t)] = sum_tile(w, 1 - h, t)
            return carry

        lax.fori_loop(0, cols // LANES, body, 0)
        final.start()

    def body(t, carry):
        med_ref[:, tile(t)] = sum_tile(w, h, t)
        return carry

    lax.fori_loop(0, cols // LANES, body, 0)
    if groups > 1:
        final.wait_recv()
        total = total + last_in[:, pl.ds(cols, LANES)]
    inverse = 1.0 / total

    def body(t, carry):
        m = med_ref[:, tile(t)]
        if groups > 1:
            m = m + last_in[:, tile(t)]
        med_ref[:, tile(t)] = m * inverse
        return carry

    lax.fori_loop(0, cols // LANES, body, 0)
    for c in range(nc):
        share = (groups * clients) * weight[pl.ds(nc * j + c, 1), :] * inverse[0:1, :]
        share_ref[c] = share[0, 0]

    for o in range(1, members):
        count_copy(o, j).wait_send()
        for k in range(chunks):
            rows_copy(o, k, j).wait_send()
    if groups > 1:
        for i in range(ITERS):
            for k in range(chunks):
                part_copy(i, k).wait_send()
        final.wait_send()


def local(updates, sample_counts):
    nc, rows, cols = updates.shape
    devices, cores = lax.axis_size("client"), lax.axis_size("param")
    groups = GROUPS if devices % GROUPS == 0 and devices > GROUPS else 1
    members = devices // groups
    tiles = cols // LANES
    bounds = sorted({0, tiles} | {round(end * tiles) for end in CHUNK_ENDS})
    chunks = len(bounds) - 1
    mine = rows // devices
    if rows % devices or mine != SUBLANES or cols % LANES or members < 2 or members & (members - 1) or nc * members > LANES:
        return local_plain(updates, sample_counts)
    clients = nc * members
    f32 = jnp.float32
    dma = pltpu.SemaphoreType.DMA
    wide = cols + LANES
    return pl.pallas_call(
        functools.partial(kernel, groups, members, cores, bounds),
        out_shape=(jax.ShapeDtypeStruct((mine, cols), f32), jax.ShapeDtypeStruct((nc,), f32)),
        in_specs=[pl.BlockSpec(memory_space=pltpu.HBM)] * 2,
        out_specs=(pl.BlockSpec(memory_space=pltpu.VMEM), pl.BlockSpec(memory_space=pltpu.SMEM)),
        scratch_shapes=[
            pltpu.VMEM((members, nc, groups, mine, cols), f32),
            pltpu.SMEM((nc,), jnp.int32),
            pltpu.VMEM((nc, LANES), f32),
            pltpu.VMEM((members, nc, LANES), f32),
            pltpu.VMEM((ITERS, 1, LANES), f32),
            pltpu.VMEM((ITERS, cores * members, 1, LANES), f32),
            pltpu.VMEM((clients, LANES), f32),
            pltpu.VMEM((clients, LANES), f32),
            pltpu.VMEM((ITERS, groups, mine, wide), f32),
            pltpu.VMEM((ITERS, groups, mine, wide), f32),
            pltpu.VMEM((mine, wide), f32),
            pltpu.VMEM((mine, wide), f32),
            dma,
            dma((chunks,)),
            dma((members, chunks)),
            dma((members, chunks)),
            dma((members,)),
            dma((members,)),
            dma((ITERS, chunks)),
            dma((ITERS, chunks)),
            dma,
            dma,
            dma((ITERS, cores * members)),
            dma((ITERS, cores * members)),
        ],
        compiler_params=pltpu.CompilerParams(
            collective_id=0, has_side_effects=True, vmem_limit_bytes=56 * 1024 * 1024),
        cost_estimate=pl.CostEstimate(
            flops=16 * clients * groups * mine * cols, bytes_accessed=8 * nc * rows * cols, transcendentals=0),
    )(updates.reshape(nc, groups, members, mine, cols), sample_counts)


def solution(mesh):
    return jax.shard_map(
        local,
        mesh=mesh,
        in_specs=(P("client", None, "param"), P("client")),
        out_specs=(P("client", "param"), P("client")),
        check_vma=False,
    )
```

```python
import functools

import jax
import jax.numpy as jnp
from jax import lax
from jax.experimental import pallas as pl
from jax.experimental.pallas import tpu as pltpu
from jax.sharding import PartitionSpec as P

ITERS = 2
LANES = 128
SUBLANES = 8
GROUPS = 2
CHUNK_ENDS = (0.43, 0.79, 1.0)

smoothing = 1e-06


def weighted_sum(weights, updates):
    return jnp.einsum("c,crk->rk", weights, updates, precision=lax.Precision.HIGHEST)


def local_plain(updates, sample_counts):
    local_clients = updates.shape[0]
    clients = local_clients * lax.axis_size("client")
    exchanged = lax.all_to_all(updates, "client", split_axis=1, concat_axis=0, tiled=True)
    counts_f = lax.all_gather(sample_counts, "client", axis=0, tiled=True).astype(jnp.float32)
    weights = counts_f
    for iteration in range(ITERS + 1):
        weight_sum = jnp.sum(weights)
        median = weighted_sum(weights, exchanged) / weight_sum
        if iteration < ITERS:
            distance_sq = jnp.sum((exchanged - median[None]) ** 2, axis=(1, 2))
            distance_sq = lax.psum(distance_sq, ("client", "param"))
            weights = counts_f / jnp.sqrt(distance_sq + smoothing)
    offset = lax.axis_index("client") * local_clients
    shares = lax.dynamic_slice_in_dim(clients * weights / weight_sum, offset, local_clients, 0)
    return (median, shares)


def kernel(groups, members, cores, bounds, u_ref, cnt_hbm, med_ref, share_ref,
           held, cnt_ref, cnt_send, cnt_held, dist_send, dist_held, dist_rows, weight, part, part_in, last, last_in,
           in_sem, own_sem, u_send, u_recv, c_send, c_recv, p_send, p_recv, l_send, l_recv, d_send, d_recv):
    nc, cols = u_ref.shape[0], u_ref.shape[-1]
    clients = nc * members
    me, core = lax.axis_index("client"), lax.axis_index("param")
    j, h = lax.rem(me, members), lax.div(me, members)
    partner = lax.rem(me + members, groups * members)
    rank = core * members + j
    chunks = len(bounds) - 1

    def lanes(k):
        return pl.ds(bounds[k] * LANES, (bounds[k + 1] - bounds[k]) * LANES)

    def member(o, c):
        return {"client": h * members + lax.rem(j + o, members), "param": lax.rem(core + c, cores)}

    others = [(o, c) for c in range(cores) for o in range(members) if o or c]
    barrier = pltpu.get_barrier_semaphore()
    for o, c in others:
        pl.semaphore_signal(barrier, inc=1, device_id=member(o, c), device_id_type=pl.DeviceIdType.MESH)
    if groups > 1:
        pl.semaphore_signal(barrier, inc=1, device_id={"client": partner}, device_id_type=pl.DeviceIdType.MESH)
    counts_in = pltpu.make_async_copy(cnt_hbm, cnt_ref, in_sem)
    counts_in.start()
    own = []
    for k in range(chunks):
        sl = lanes(k)
        own.append(pltpu.make_async_copy(u_ref.at[:, :, j, :, sl], held.at[j, :, :, :, sl], own_sem.at[k]))
        own[-1].start()
    pl.semaphore_wait(barrier, len(others) + (groups > 1))

    full = members - 1
    masks = [m for low in range(1, members // 2) for m in (low, full - low)] + [full]
    bits = [1 << b for b in range(full.bit_length())]

    def peer(o):
        m, index = masks[o - 1], 0
        for b in bits:
            flip = (m // b) % 2
            if m != full:
                flip = flip + lax.rem(core, 2) * (1 - 2 * flip)
            index = index + b * lax.rem(lax.rem(lax.div(j, b), 2) + flip, 2)
        return index

    def count_copy(o, slot):
        return pltpu.make_async_remote_copy(
            src_ref=cnt_send, dst_ref=cnt_held.at[slot], send_sem=c_send.at[o], recv_sem=c_recv.at[o],
            device_id={"client": h * members + peer(o)}, device_id_type=pl.DeviceIdType.MESH)

    def rows_copy(o, k, slot):
        to = peer(o)
        sl = lanes(k)
        return pltpu.make_async_remote_copy(
            src_ref=u_ref.at[:, :, to, :, sl], dst_ref=held.at[slot, :, :, :, sl],
            send_sem=u_send.at[o, k], recv_sem=u_recv.at[o, k],
            device_id={"client": h * members + to}, device_id_type=pl.DeviceIdType.MESH)

    def source(o):
        return lax.rem(j + members - o, members)

    for k in range(chunks):
        for o in range(1, members):
            rows_copy(o, k, j).start()
        if k == 0:
            counts_in.wait()
            for c in range(nc):
                row = jnp.full((1, LANES), cnt_ref[c], jnp.int32).astype(jnp.float32)
                cnt_send[c:c + 1, :] = row
                cnt_held[j, c:c + 1, :] = row
            for o in range(1, members):
                count_copy(o, j).start()

    def part_copy(i, k):
        first = bounds[k] + (k > 0)
        sl = pl.ds(first * LANES, (bounds[k + 1] + 1 - first) * LANES)
        return pltpu.make_async_remote_copy(
            src_ref=part.at[i, :, :, sl], dst_ref=part_in.at[i, :, :, sl],
            send_sem=p_send.at[i, k], recv_sem=p_recv.at[i, k],
            device_id={"client": partner}, device_id_type=pl.DeviceIdType.MESH)

    def dist_copy(i, n, o, c, slot):
        return pltpu.make_async_remote_copy(
            src_ref=dist_send.at[i], dst_ref=dist_held.at[i, slot],
            send_sem=d_send.at[i, n], recv_sem=d_recv.at[i, n],
            device_id=member(o, c), device_id_type=pl.DeviceIdType.MESH)

    def weights_now():
        w = [jnp.broadcast_to(weight[c:c + 1, :], (SUBLANES, LANES)) for c in range(clients)]
        total = w[0]
        for x in w[1:]:
            total = total + x
        return w, total

    def tile(t):
        return pl.ds(pl.multiple_of(t * LANES, LANES), LANES)

    def after(t):
        return pl.ds(pl.multiple_of((t + 1) * LANES, LANES), LANES)

    def sum_tile(w, r, t):
        sums = []
        for c in range(clients):
            x = w[c] * held[c // nc, c % nc, r, :, tile(t)]
            if c < 4:
                sums.append(x)
            else:
                sums[c % 4] = sums[c % 4] + x
        while len(sums) > 1:
            sums = [sums[n] + sums[n + 1] if n + 1 < len(sums) else sums[n] for n in range(0, len(sums), 2)]
        return sums[0]

    def iteration(i):
        w, total = weights_now()
        for r in range(groups):
            part[i, r, :, pl.ds(0, LANES)] = total

        def send_part(k):
            def body(t, carry):
                for r in range(groups):
                    part[i, r, :, after(t)] = sum_tile(w, r, t)
                return carry

            lax.fori_loop(bounds[k], bounds[k + 1], body, 0)
            if groups > 1:
                part_copy(i, k).start()

        def add_distances(k, inverse, acc):
            if groups > 1:
                part_copy(i, k).wait_recv()
            if inverse is None:
                whole = part[i, 0, :, pl.ds(0, LANES)]
                if groups > 1:
                    whole = whole + part_in[i, 0, :, pl.ds(0, LANES)]
                inverse = 1.0 / whole

            def body(t, acc):
                acc = list(acc)
                for r in range(groups):
                    m = part[i, r, :, after(t)]
                    if groups > 1:
                        m = m + part_in[i, r, :, after(t)]
                    m = m * inverse
                    for c in range(clients):
                        d = held[c // nc, c % nc, r, :, tile(t)] - m
                        acc[c] = acc[c] + d * d
                return tuple(acc)

            return inverse, lax.fori_loop(bounds[k], bounds[k + 1], body, acc)

        inverse, acc = None, tuple(jnp.zeros((SUBLANES, LANES), jnp.float32) for _ in range(clients))
        for k in range(chunks):
            if i == 0:
                own[k].wait()
                for o in range(1, members):
                    rows_copy(o, k, peer(o)).wait_recv()
            send_part(k)
            if i == 0 and k > 0:
                inverse, acc = add_distances(k - 1, inverse, acc)
        if i == 1:
            for o in range(1, members):
                count_copy(o, j).wait_send()
                for k in range(chunks):
                    rows_copy(o, k, j).wait_send()
        if i > 0:
            for n, (o, c) in enumerate(others):
                dist_copy(i - 1, n, o, c, rank).wait_send()
        for k in range(chunks - 1 if i == 0 else 0, chunks):
            inverse, acc = add_distances(k, inverse, acc)
        for c in range(clients):
            dist_rows[c:c + 1, :] = jnp.sum(acc[c], axis=0, keepdims=True)
        eye = (lax.broadcasted_iota(jnp.int32, (clients, LANES), 0)
               == lax.broadcasted_iota(jnp.int32, (clients, LANES), 1))
        column = jnp.sum(dist_rows[...], axis=1, keepdims=True)
        row = jnp.sum(jnp.where(eye, column, 0.0), axis=0, keepdims=True)
        dist_send[i] = row
        dist_held[i, rank] = row

        for n, (o, c) in enumerate(others):
            dist_copy(i, n, o, c, rank).start()
        for n, (o, c) in enumerate(others):
            dist_copy(i, n, o, c, lax.rem(core + cores - c, cores) * members + source(o)).wait_recv()
        row = dist_held[i, 0]
        for s in range(1, cores * members):
            row = row + dist_held[i, s]
        column = jnp.sum(jnp.where(eye, jnp.broadcast_to(row, eye.shape), 0.0), axis=1, keepdims=True)
        root = jnp.sqrt(jnp.broadcast_to(column, eye.shape) + smoothing)
        for c in range(clients):
            weight[c:c + 1, :] = cnt_held[c // nc, c % nc:c % nc + 1, :] / root[c:c + 1, :]

    for o in range(1, members):
        count_copy(o, peer(o)).wait_recv()
    for c in range(clients):
        weight[c:c + 1, :] = cnt_held[c // nc, c % nc:c % nc + 1, :]
    for i in range(ITERS):
        iteration(i)

    w, total = weights_now()
    final = pltpu.make_async_remote_copy(
        src_ref=last, dst_ref=last_in, send_sem=l_send, recv_sem=l_recv,
        device_id={"client": partner}, device_id_type=pl.DeviceIdType.MESH)
    if groups > 1:
        last[:, pl.ds(0, LANES)] = total

        def body(t, carry):
            last[:, after(t)] = sum_tile(w, 1 - h, t)
            return carry

        lax.fori_loop(0, cols // LANES, body, 0)
        final.start()

    def body(t, carry):
        med_ref[:, tile(t)] = sum_tile(w, h, t)
        return carry

    lax.fori_loop(0, cols // LANES, body, 0)
    for n, (o, c) in enumerate(others):
        dist_copy(ITERS - 1, n, o, c, rank).wait_send()
    if groups > 1:
        for i in range(ITERS):
            for k in range(chunks):
                part_copy(i, k).wait_send()
        final.wait_recv()
        total = total + last_in[:, pl.ds(0, LANES)]
    inverse = 1.0 / total

    def body(t, carry):
        m = med_ref[:, tile(t)]
        if groups > 1:
            m = m + last_in[:, after(t)]
        med_ref[:, tile(t)] = m * inverse
        return carry

    lax.fori_loop(0, cols // LANES, body, 0)
    for c in range(nc):
        share = (groups * clients) * weight[pl.ds(nc * j + c, 1), :] * inverse[0:1, :]
        share_ref[c] = share[0, 0]
    if groups > 1:
        final.wait_send()


def local(updates, sample_counts):
    nc, rows, cols = updates.shape
    devices, cores = lax.axis_size("client"), lax.axis_size("param")
    groups = GROUPS if devices % GROUPS == 0 and devices > GROUPS else 1
    members = devices // groups
    tiles = cols // LANES
    bounds = sorted({0, tiles} | {round(end * tiles) for end in CHUNK_ENDS})
    chunks = len(bounds) - 1
    mine = rows // devices
    if rows % devices or mine != SUBLANES or cols % LANES or members < 2 or members & (members - 1) or nc * members > LANES:
        return local_plain(updates, sample_counts)
    clients = nc * members
    f32 = jnp.float32
    dma = pltpu.SemaphoreType.DMA
    wide = cols + LANES
    return pl.pallas_call(
        functools.partial(kernel, groups, members, cores, bounds),
        out_shape=(pltpu.VMEM((mine, cols), f32), pltpu.SMEM((nc,), f32)),
        in_specs=[pl.BlockSpec(memory_space=pltpu.HBM)] * 2,
        out_specs=(pl.BlockSpec(memory_space=pltpu.VMEM), pl.BlockSpec(memory_space=pltpu.SMEM)),
        scratch_shapes=[
            pltpu.VMEM((members, nc, groups, mine, cols), f32),
            pltpu.SMEM((nc,), jnp.int32),
            pltpu.VMEM((nc, LANES), f32),
            pltpu.VMEM((members, nc, LANES), f32),
            pltpu.VMEM((ITERS, 1, LANES), f32),
            pltpu.VMEM((ITERS, cores * members, 1, LANES), f32),
            pltpu.VMEM((clients, LANES), f32),
            pltpu.VMEM((clients, LANES), f32),
            pltpu.VMEM((ITERS, groups, mine, wide), f32),
            pltpu.VMEM((ITERS, groups, mine, wide), f32),
            pltpu.VMEM((mine, wide), f32),
            pltpu.VMEM((mine, wide), f32),
            dma,
            dma((chunks,)),
            dma((members, chunks)),
            dma((members, chunks)),
            dma((members,)),
            dma((members,)),
            dma((ITERS, chunks)),
            dma((ITERS, chunks)),
            dma,
            dma,
            dma((ITERS, cores * members)),
            dma((ITERS, cores * members)),
        ],
        compiler_params=pltpu.CompilerParams(
            collective_id=0, has_side_effects=True, vmem_limit_bytes=56 * 1024 * 1024),
        cost_estimate=pl.CostEstimate(
            flops=16 * clients * groups * mine * cols, bytes_accessed=8 * nc * rows * cols, transcendentals=0),
    )(updates.reshape(nc, groups, members, mine, cols), sample_counts)


def solution(mesh):
    return jax.shard_map(
        local,
        mesh=mesh,
        in_specs=(P("client", None, "param"), P("client")),
        out_specs=(P("client", "param"), P("client")),
        check_vma=False,
    )
```

```python
import functools

import jax
import jax.numpy as jnp
from jax import lax
from jax.experimental import pallas as pl
from jax.experimental.pallas import tpu as pltpu
from jax.sharding import PartitionSpec as P

ITERS = 2
LANES = 128
SUBLANES = 8
GROUPS = 2
CHUNK_ENDS = (0.5, 0.79, 0.93, 1.0)
LAST_ENDS = (0.43, 1.0)

smoothing = 1e-06


def weighted_sum(weights, updates):
    return jnp.einsum("c,crk->rk", weights, updates, precision=lax.Precision.HIGHEST)


def local_plain(updates, sample_counts):
    local_clients = updates.shape[0]
    clients = local_clients * lax.axis_size("client")
    exchanged = lax.all_to_all(updates, "client", split_axis=1, concat_axis=0, tiled=True)
    counts_f = lax.all_gather(sample_counts, "client", axis=0, tiled=True).astype(jnp.float32)
    weights = counts_f
    for iteration in range(ITERS + 1):
        weight_sum = jnp.sum(weights)
        median = weighted_sum(weights, exchanged) / weight_sum
        if iteration < ITERS:
            distance_sq = jnp.sum((exchanged - median[None]) ** 2, axis=(1, 2))
            distance_sq = lax.psum(distance_sq, ("client", "param"))
            weights = counts_f / jnp.sqrt(distance_sq + smoothing)
    offset = lax.axis_index("client") * local_clients
    shares = lax.dynamic_slice_in_dim(clients * weights / weight_sum, offset, local_clients, 0)
    return (median, shares)


def kernel(groups, members, cores, bounds, ends, u_ref, cnt_hbm, med_ref, share_ref,
           held, cnt_ref, cnt_send, cnt_held, dist_send, dist_held, dist_rows, weight, part, part_in, last, last_in,
           in_sem, own_sem, u_send, u_recv, c_send, c_recv, p_send, p_recv, l_send, l_recv, d_send, d_recv):
    nc, cols = u_ref.shape[0], u_ref.shape[-1]
    clients = nc * members
    me, core = lax.axis_index("client"), lax.axis_index("param")
    j, h = lax.rem(me, members), lax.div(me, members)
    partner = lax.rem(me + members, groups * members)
    rank = core * members + j
    chunks = len(bounds) - 1

    def lanes(k):
        return pl.ds(bounds[k] * LANES, (bounds[k + 1] - bounds[k]) * LANES)

    def member(o, c):
        return {"client": h * members + flipped(o), "param": lax.rem(core + c, cores)}

    def flipped(m):
        return sum(b * lax.rem(lax.rem(lax.div(j, b), 2) + (m // b) % 2, 2) for b in bits)

    full = members - 1
    bits = [1 << b for b in range(full.bit_length())]
    others = sorted(((o, c) for c in range(cores) for o in range(members) if o or c),
                    key=lambda x: -bin(x[0]).count("1"))
    barrier = pltpu.get_barrier_semaphore()
    for o, c in others:
        pl.semaphore_signal(barrier, inc=1, device_id=member(o, c), device_id_type=pl.DeviceIdType.MESH)
    if groups > 1:
        pl.semaphore_signal(barrier, inc=1, device_id={"client": partner}, device_id_type=pl.DeviceIdType.MESH)
    counts_in = pltpu.make_async_copy(cnt_hbm, cnt_ref, in_sem)
    counts_in.start()
    own = []
    for k in range(chunks):
        sl = lanes(k)
        own.append(pltpu.make_async_copy(u_ref.at[:, :, j, :, sl], held.at[j, :, :, :, sl], own_sem.at[k]))
        own[-1].start()
    pl.semaphore_wait(barrier, len(others) + (groups > 1))

    masks = [full] + [m for low in range(members // 2 - 1, 0, -1) for m in (full - low, low)]

    def peer(o):
        m, index = masks[o - 1], 0
        for b in bits:
            flip = (m // b) % 2
            if m != full:
                flip = flip + lax.rem(core, 2) * (1 - 2 * flip)
            index = index + b * lax.rem(lax.rem(lax.div(j, b), 2) + flip, 2)
        return index

    def count_copy(o, slot):
        return pltpu.make_async_remote_copy(
            src_ref=cnt_send, dst_ref=cnt_held.at[slot], send_sem=c_send.at[o], recv_sem=c_recv.at[o],
            device_id={"client": h * members + peer(o)}, device_id_type=pl.DeviceIdType.MESH)

    def rows_copy(o, k, slot):
        to = peer(o)
        sl = lanes(k)
        return pltpu.make_async_remote_copy(
            src_ref=u_ref.at[:, :, to, :, sl], dst_ref=held.at[slot, :, :, :, sl],
            send_sem=u_send.at[o, k], recv_sem=u_recv.at[o, k],
            device_id={"client": h * members + to}, device_id_type=pl.DeviceIdType.MESH)

    for k in range(chunks):
        for o in range(1, members):
            rows_copy(o, k, j).start()
        if k == 0:
            counts_in.wait()
            for c in range(nc):
                row = jnp.full((1, LANES), cnt_ref[c], jnp.int32).astype(jnp.float32)
                cnt_send[c:c + 1, :] = row
                cnt_held[j, c:c + 1, :] = row
            for o in range(1, members):
                count_copy(o, j).start()

    def part_copy(i, k):
        first = bounds[k] + (k > 0)
        sl = pl.ds(first * LANES, (bounds[k + 1] + 1 - first) * LANES)
        return pltpu.make_async_remote_copy(
            src_ref=part.at[i, :, :, sl], dst_ref=part_in.at[i, :, :, sl],
            send_sem=p_send.at[i, k], recv_sem=p_recv.at[i, k],
            device_id={"client": partner}, device_id_type=pl.DeviceIdType.MESH)

    def dist_copy(i, n, o, c, slot):
        return pltpu.make_async_remote_copy(
            src_ref=dist_send.at[i], dst_ref=dist_held.at[i, slot],
            send_sem=d_send.at[i, n], recv_sem=d_recv.at[i, n],
            device_id=member(o, c), device_id_type=pl.DeviceIdType.MESH)

    def weights_now():
        w = [jnp.broadcast_to(weight[c:c + 1, :], (SUBLANES, LANES)) for c in range(clients)]
        total = w[0]
        for x in w[1:]:
            total = total + x
        return w, total

    def tile(t):
        return pl.ds(pl.multiple_of(t * LANES, LANES), LANES)

    def after(t):
        return pl.ds(pl.multiple_of((t + 1) * LANES, LANES), LANES)

    def sum_tile(w, r, t):
        sums = []
        for c in range(clients):
            x = w[c] * held[c // nc, c % nc, r, :, tile(t)]
            if c < 4:
                sums.append(x)
            else:
                sums[c % 4] = sums[c % 4] + x
        while len(sums) > 1:
            sums = [sums[n] + sums[n + 1] if n + 1 < len(sums) else sums[n] for n in range(0, len(sums), 2)]
        return sums[0]

    def iteration(i):
        w, total = weights_now()
        for r in range(groups):
            part[i, r, :, pl.ds(0, LANES)] = total

        def send_part(k):
            def body(t, carry):
                for r in range(groups):
                    part[i, r, :, after(t)] = sum_tile(w, r, t)
                return carry

            lax.fori_loop(bounds[k], bounds[k + 1], body, 0)
            if groups > 1:
                part_copy(i, k).start()

        def add_distances(k, inverse, acc):
            if groups > 1:
                part_copy(i, k).wait_recv()
            if inverse is None:
                whole = part[i, 0, :, pl.ds(0, LANES)]
                if groups > 1:
                    whole = whole + part_in[i, 0, :, pl.ds(0, LANES)]
                inverse = 1.0 / whole

            def body(t, acc):
                acc = list(acc)
                for r in range(groups):
                    m = part[i, r, :, after(t)]
                    if groups > 1:
                        m = m + part_in[i, r, :, after(t)]
                    m = m * inverse
                    for c in range(clients):
                        d = held[c // nc, c % nc, r, :, tile(t)] - m
                        acc[c] = acc[c] + d * d
                return tuple(acc)

            return inverse, lax.fori_loop(bounds[k], bounds[k + 1], body, acc)

        inverse, acc = None, tuple(jnp.zeros((SUBLANES, LANES), jnp.float32) for _ in range(clients))
        for k in range(chunks):
            if i == 0:
                own[k].wait()
                for o in range(1, members):
                    rows_copy(o, k, peer(o)).wait_recv()
            send_part(k)
            if i == 0 and k > 0:
                inverse, acc = add_distances(k - 1, inverse, acc)
        if i == 1:
            for o in range(1, members):
                count_copy(o, j).wait_send()
                for k in range(chunks):
                    rows_copy(o, k, j).wait_send()
        if i > 0:
            for n, (o, c) in enumerate(others):
                dist_copy(i - 1, n, o, c, rank).wait_send()
        for k in range(chunks - 1 if i == 0 else 0, chunks):
            inverse, acc = add_distances(k, inverse, acc)
        for c in range(clients):
            dist_rows[c:c + 1, :] = jnp.sum(acc[c], axis=0, keepdims=True)
        eye = (lax.broadcasted_iota(jnp.int32, (clients, LANES), 0)
               == lax.broadcasted_iota(jnp.int32, (clients, LANES), 1))
        column = jnp.sum(dist_rows[...], axis=1, keepdims=True)
        row = jnp.sum(jnp.where(eye, column, 0.0), axis=0, keepdims=True)
        dist_send[i] = row
        dist_held[i, rank] = row

        for n, (o, c) in enumerate(others):
            dist_copy(i, n, o, c, rank).start()
        for n, (o, c) in enumerate(others):
            dist_copy(i, n, o, c, lax.rem(core + cores - c, cores) * members + flipped(o)).wait_recv()
        row = dist_held[i, 0]
        for s in range(1, cores * members):
            row = row + dist_held[i, s]
        column = jnp.sum(jnp.where(eye, jnp.broadcast_to(row, eye.shape), 0.0), axis=1, keepdims=True)
        root = jnp.sqrt(jnp.broadcast_to(column, eye.shape) + smoothing)
        for c in range(clients):
            weight[c:c + 1, :] = cnt_held[c // nc, c % nc:c % nc + 1, :] / root[c:c + 1, :]

    for o in range(1, members):
        count_copy(o, peer(o)).wait_recv()
    for c in range(clients):
        weight[c:c + 1, :] = cnt_held[c // nc, c % nc:c % nc + 1, :]
    for i in range(ITERS):
        iteration(i)

    w, total = weights_now()
    def final_copy(k):
        first = ends[k] + (k > 0)
        sl = pl.ds(first * LANES, (ends[k + 1] + 1 - first) * LANES)
        return pltpu.make_async_remote_copy(
            src_ref=last.at[:, sl], dst_ref=last_in.at[:, sl], send_sem=l_send.at[k], recv_sem=l_recv.at[k],
            device_id={"client": partner}, device_id_type=pl.DeviceIdType.MESH)

    if groups > 1:
        last[:, pl.ds(0, LANES)] = total

        def body(t, carry):
            last[:, after(t)] = sum_tile(w, 1 - h, t)
            return carry

        for k in range(len(ends) - 1):
            lax.fori_loop(ends[k], ends[k + 1], body, 0)
            final_copy(k).start()

    def body(t, carry):
        med_ref[:, tile(t)] = sum_tile(w, h, t)
        return carry

    lax.fori_loop(0, cols // LANES, body, 0)
    for n, (o, c) in enumerate(others):
        dist_copy(ITERS - 1, n, o, c, rank).wait_send()
    if groups > 1:
        for i in range(ITERS):
            for k in range(chunks):
                part_copy(i, k).wait_send()
        final_copy(0).wait_recv()
        total = total + last_in[:, pl.ds(0, LANES)]
    inverse = 1.0 / total

    def body(t, carry):
        m = med_ref[:, tile(t)]
        if groups > 1:
            m = m + last_in[:, after(t)]
        med_ref[:, tile(t)] = m * inverse
        return carry

    for k in range(len(ends) - 1):
        if groups > 1 and k > 0:
            final_copy(k).wait_recv()
        lax.fori_loop(ends[k], ends[k + 1], body, 0)
    for c in range(nc):
        share = (groups * clients) * weight[pl.ds(nc * j + c, 1), :] * inverse[0:1, :]
        share_ref[c] = share[0, 0]
    if groups > 1:
        for k in range(len(ends) - 1):
            final_copy(k).wait_send()


def local(updates, sample_counts):
    nc, rows, cols = updates.shape
    devices, cores = lax.axis_size("client"), lax.axis_size("param")
    groups = GROUPS if devices % GROUPS == 0 and devices > GROUPS else 1
    members = devices // groups
    tiles = cols // LANES
    bounds = sorted({0, tiles} | {round(end * tiles) for end in CHUNK_ENDS})
    ends = sorted({0, tiles} | {round(end * tiles) for end in LAST_ENDS})
    chunks = len(bounds) - 1
    mine = rows // devices
    if rows % devices or mine != SUBLANES or cols % LANES or members < 2 or members & (members - 1) or nc * members > LANES:
        return local_plain(updates, sample_counts)
    clients = nc * members
    f32 = jnp.float32
    dma = pltpu.SemaphoreType.DMA
    wide = cols + LANES
    return pl.pallas_call(
        functools.partial(kernel, groups, members, cores, bounds, ends),
        out_shape=(pltpu.VMEM((mine, cols), f32), pltpu.SMEM((nc,), f32)),
        in_specs=[pl.BlockSpec(memory_space=pltpu.HBM)] * 2,
        out_specs=(pl.BlockSpec(memory_space=pltpu.VMEM), pl.BlockSpec(memory_space=pltpu.SMEM)),
        scratch_shapes=[
            pltpu.VMEM((members, nc, groups, mine, cols), f32),
            pltpu.SMEM((nc,), jnp.int32),
            pltpu.VMEM((nc, LANES), f32),
            pltpu.VMEM((members, nc, LANES), f32),
            pltpu.VMEM((ITERS, 1, LANES), f32),
            pltpu.VMEM((ITERS, cores * members, 1, LANES), f32),
            pltpu.VMEM((clients, LANES), f32),
            pltpu.VMEM((clients, LANES), f32),
            pltpu.VMEM((ITERS, groups, mine, wide), f32),
            pltpu.VMEM((ITERS, groups, mine, wide), f32),
            pltpu.VMEM((mine, wide), f32),
            pltpu.VMEM((mine, wide), f32),
            dma,
            dma((chunks,)),
            dma((members, chunks)),
            dma((members, chunks)),
            dma((members,)),
            dma((members,)),
            dma((ITERS, chunks)),
            dma((ITERS, chunks)),
            dma((len(ends) - 1,)),
            dma((len(ends) - 1,)),
            dma((ITERS, cores * members)),
            dma((ITERS, cores * members)),
        ],
        compiler_params=pltpu.CompilerParams(
            collective_id=0, has_side_effects=True, vmem_limit_bytes=56 * 1024 * 1024),
        cost_estimate=pl.CostEstimate(
            flops=16 * clients * groups * mine * cols, bytes_accessed=8 * nc * rows * cols, transcendentals=0),
    )(updates.reshape(nc, groups, members, mine, cols), sample_counts)


def solution(mesh):
    return jax.shard_map(
        local,
        mesh=mesh,
        in_specs=(P("client", None, "param"), P("client")),
        out_specs=(P("client", "param"), P("client")),
        check_vma=False,
    )
```

```python
import functools

import jax
import jax.numpy as jnp
from jax import lax
from jax.experimental import pallas as pl
from jax.experimental.pallas import tpu as pltpu
from jax.sharding import PartitionSpec as P

ITERS = 2
LANES = 128
SUBLANES = 8
GROUPS = 2
CHUNK_TILES = 2
IN_FLIGHT = 3
LAST_ENDS = (0.43, 1.0)

smoothing = 1e-06


def weighted_sum(weights, updates):
    return jnp.einsum("c,crk->rk", weights, updates, precision=lax.Precision.HIGHEST)


def local_plain(updates, sample_counts):
    local_clients = updates.shape[0]
    clients = local_clients * lax.axis_size("client")
    exchanged = lax.all_to_all(updates, "client", split_axis=1, concat_axis=0, tiled=True)
    counts_f = lax.all_gather(sample_counts, "client", axis=0, tiled=True).astype(jnp.float32)
    weights = counts_f
    for iteration in range(ITERS + 1):
        weight_sum = jnp.sum(weights)
        median = weighted_sum(weights, exchanged) / weight_sum
        if iteration < ITERS:
            distance_sq = jnp.sum((exchanged - median[None]) ** 2, axis=(1, 2))
            distance_sq = lax.psum(distance_sq, ("client", "param"))
            weights = counts_f / jnp.sqrt(distance_sq + smoothing)
    offset = lax.axis_index("client") * local_clients
    shares = lax.dynamic_slice_in_dim(clients * weights / weight_sum, offset, local_clients, 0)
    return (median, shares)


def kernel(groups, members, cores, bounds, ends, u_ref, cnt_hbm, med_ref, share_ref,
           held, cnt_ref, cnt_send, cnt_held, dist_send, dist_held, dist_rows, weight, part, part_in, last, last_in,
           in_sem, own_sem, u_send, u_recv, c_send, c_recv, p_send, p_recv, l_send, l_recv, d_send, d_recv):
    nc, cols = u_ref.shape[0], u_ref.shape[-1]
    clients = nc * members
    me, core = lax.axis_index("client"), lax.axis_index("param")
    j, h = lax.rem(me, members), lax.div(me, members)
    partner = lax.rem(me + members, groups * members)
    rank = core * members + j
    chunks = len(bounds) - 1

    def lanes(k):
        return pl.ds(bounds[k] * LANES, (bounds[k + 1] - bounds[k]) * LANES)

    def member(o, c):
        return {"client": h * members + flipped(o), "param": lax.rem(core + c, cores)}

    def flipped(m):
        return sum(b * lax.rem(lax.rem(lax.div(j, b), 2) + (m // b) % 2, 2) for b in bits)

    full = members - 1
    bits = [1 << b for b in range(full.bit_length())]
    others = sorted(((o, c) for c in range(cores) for o in range(members) if o or c),
                    key=lambda x: -bin(x[0]).count("1"))
    barrier = pltpu.get_barrier_semaphore()
    for o, c in others:
        pl.semaphore_signal(barrier, inc=1, device_id=member(o, c), device_id_type=pl.DeviceIdType.MESH)
    if groups > 1:
        pl.semaphore_signal(barrier, inc=1, device_id={"client": partner}, device_id_type=pl.DeviceIdType.MESH)
    counts_in = pltpu.make_async_copy(cnt_hbm, cnt_ref, in_sem)
    counts_in.start()
    own = []
    for k in range(chunks):
        sl = lanes(k)
        own.append(pltpu.make_async_copy(u_ref.at[:, :, j, :, sl], held.at[j, :, :, :, sl], own_sem.at[k]))
        own[-1].start()
    pl.semaphore_wait(barrier, len(others) + (groups > 1))

    masks = [full] + [m for low in range(members // 2 - 1, 0, -1) for m in (full - low, low)]

    def peer(o):
        m, index = masks[o - 1], 0
        for b in bits:
            flip = (m // b) % 2
            if m != full:
                flip = flip + lax.rem(core, 2) * (1 - 2 * flip)
            index = index + b * lax.rem(lax.rem(lax.div(j, b), 2) + flip, 2)
        return index

    def count_copy(o, slot):
        return pltpu.make_async_remote_copy(
            src_ref=cnt_send, dst_ref=cnt_held.at[slot], send_sem=c_send.at[o], recv_sem=c_recv.at[o],
            device_id={"client": h * members + peer(o)}, device_id_type=pl.DeviceIdType.MESH)

    def rows_copy(o, k, slot):
        to = peer(o)
        sl = lanes(k)
        return pltpu.make_async_remote_copy(
            src_ref=u_ref.at[:, :, to, :, sl], dst_ref=held.at[slot, :, :, :, sl],
            send_sem=u_send.at[o, k], recv_sem=u_recv.at[o, k],
            device_id={"client": h * members + to}, device_id_type=pl.DeviceIdType.MESH)

    for k in range(min(IN_FLIGHT, chunks)):
        for o in range(1, members):
            rows_copy(o, k, j).start()
        if k == 0:
            counts_in.wait()
            for c in range(nc):
                row = jnp.full((1, LANES), cnt_ref[c], jnp.int32).astype(jnp.float32)
                cnt_send[c:c + 1, :] = row
                cnt_held[j, c:c + 1, :] = row
            for o in range(1, members):
                count_copy(o, j).start()

    def part_copy(i, k):
        first = bounds[k] + (k > 0)
        sl = pl.ds(first * LANES, (bounds[k + 1] + 1 - first) * LANES)
        return pltpu.make_async_remote_copy(
            src_ref=part.at[i, :, :, sl], dst_ref=part_in.at[i, :, :, sl],
            send_sem=p_send.at[i, k], recv_sem=p_recv.at[i, k],
            device_id={"client": partner}, device_id_type=pl.DeviceIdType.MESH)

    def dist_copy(i, n, o, c, slot):
        return pltpu.make_async_remote_copy(
            src_ref=dist_send.at[i], dst_ref=dist_held.at[i, slot],
            send_sem=d_send.at[i, n], recv_sem=d_recv.at[i, n],
            device_id=member(o, c), device_id_type=pl.DeviceIdType.MESH)

    def weights_now():
        w = [jnp.broadcast_to(weight[c:c + 1, :], (SUBLANES, LANES)) for c in range(clients)]
        total = w[0]
        for x in w[1:]:
            total = total + x
        return w, total

    def tile(t):
        return pl.ds(pl.multiple_of(t * LANES, LANES), LANES)

    def after(t):
        return pl.ds(pl.multiple_of((t + 1) * LANES, LANES), LANES)

    def sum_tile(w, r, t):
        sums = []
        for c in range(clients):
            x = w[c] * held[c // nc, c % nc, r, :, tile(t)]
            if c < 4:
                sums.append(x)
            else:
                sums[c % 4] = sums[c % 4] + x
        while len(sums) > 1:
            sums = [sums[n] + sums[n + 1] if n + 1 < len(sums) else sums[n] for n in range(0, len(sums), 2)]
        return sums[0]

    def iteration(i):
        w, total = weights_now()
        for r in range(groups):
            part[i, r, :, pl.ds(0, LANES)] = total

        def send_part(k):
            def body(t, carry):
                for r in range(groups):
                    part[i, r, :, after(t)] = sum_tile(w, r, t)
                return carry

            lax.fori_loop(bounds[k], bounds[k + 1], body, 0)
            if groups > 1:
                part_copy(i, k).start()

        def add_distances(k, inverse, acc):
            if groups > 1:
                part_copy(i, k).wait_recv()
            if inverse is None:
                whole = part[i, 0, :, pl.ds(0, LANES)]
                if groups > 1:
                    whole = whole + part_in[i, 0, :, pl.ds(0, LANES)]
                inverse = 1.0 / whole

            def body(t, acc):
                acc = list(acc)
                for r in range(groups):
                    m = part[i, r, :, after(t)]
                    if groups > 1:
                        m = m + part_in[i, r, :, after(t)]
                    m = m * inverse
                    for c in range(clients):
                        d = held[c // nc, c % nc, r, :, tile(t)] - m
                        acc[c] = acc[c] + d * d
                return tuple(acc)

            return inverse, lax.fori_loop(bounds[k], bounds[k + 1], body, acc)

        inverse, acc = None, tuple(jnp.zeros((SUBLANES, LANES), jnp.float32) for _ in range(clients))
        for k in range(chunks):
            if i == 0:
                own[k].wait()
                for o in range(1, members):
                    rows_copy(o, k, peer(o)).wait_recv()
                    if k + IN_FLIGHT < chunks:
                        rows_copy(o, k + IN_FLIGHT, j).start()
            send_part(k)
            if i == 0 and k > 0:
                inverse, acc = add_distances(k - 1, inverse, acc)
        if i == 1:
            for o in range(1, members):
                count_copy(o, j).wait_send()
                for k in range(chunks):
                    rows_copy(o, k, j).wait_send()
        if i > 0:
            for n, (o, c) in enumerate(others):
                dist_copy(i - 1, n, o, c, rank).wait_send()
        for k in range(chunks - 1 if i == 0 else 0, chunks):
            inverse, acc = add_distances(k, inverse, acc)
        for c in range(clients):
            dist_rows[c:c + 1, :] = jnp.sum(acc[c], axis=0, keepdims=True)
        eye = (lax.broadcasted_iota(jnp.int32, (clients, LANES), 0)
               == lax.broadcasted_iota(jnp.int32, (clients, LANES), 1))
        column = jnp.sum(dist_rows[...], axis=1, keepdims=True)
        row = jnp.sum(jnp.where(eye, column, 0.0), axis=0, keepdims=True)
        dist_send[i] = row
        dist_held[i, rank] = row

        for n, (o, c) in enumerate(others):
            dist_copy(i, n, o, c, rank).start()
        for n, (o, c) in enumerate(others):
            dist_copy(i, n, o, c, lax.rem(core + cores - c, cores) * members + flipped(o)).wait_recv()
        row = dist_held[i, 0]
        for s in range(1, cores * members):
            row = row + dist_held[i, s]
        column = jnp.sum(jnp.where(eye, jnp.broadcast_to(row, eye.shape), 0.0), axis=1, keepdims=True)
        root = jnp.sqrt(jnp.broadcast_to(column, eye.shape) + smoothing)
        for c in range(clients):
            weight[c:c + 1, :] = cnt_held[c // nc, c % nc:c % nc + 1, :] / root[c:c + 1, :]

    for o in range(1, members):
        count_copy(o, peer(o)).wait_recv()
    for c in range(clients):
        weight[c:c + 1, :] = cnt_held[c // nc, c % nc:c % nc + 1, :]
    for i in range(ITERS):
        iteration(i)

    w, total = weights_now()
    def final_copy(k):
        first = ends[k] + (k > 0)
        sl = pl.ds(first * LANES, (ends[k + 1] + 1 - first) * LANES)
        return pltpu.make_async_remote_copy(
            src_ref=last.at[:, sl], dst_ref=last_in.at[:, sl], send_sem=l_send.at[k], recv_sem=l_recv.at[k],
            device_id={"client": partner}, device_id_type=pl.DeviceIdType.MESH)

    if groups > 1:
        last[:, pl.ds(0, LANES)] = total

        def body(t, carry):
            last[:, after(t)] = sum_tile(w, 1 - h, t)
            return carry

        for k in range(len(ends) - 1):
            lax.fori_loop(ends[k], ends[k + 1], body, 0)
            final_copy(k).start()

    def body(t, carry):
        med_ref[:, tile(t)] = sum_tile(w, h, t)
        return carry

    lax.fori_loop(0, cols // LANES, body, 0)
    for n, (o, c) in enumerate(others):
        dist_copy(ITERS - 1, n, o, c, rank).wait_send()
    if groups > 1:
        for i in range(ITERS):
            for k in range(chunks):
                part_copy(i, k).wait_send()
        final_copy(0).wait_recv()
        total = total + last_in[:, pl.ds(0, LANES)]
    inverse = 1.0 / total

    def body(t, carry):
        m = med_ref[:, tile(t)]
        if groups > 1:
            m = m + last_in[:, after(t)]
        med_ref[:, tile(t)] = m * inverse
        return carry

    for k in range(len(ends) - 1):
        if groups > 1 and k > 0:
            final_copy(k).wait_recv()
        lax.fori_loop(ends[k], ends[k + 1], body, 0)
    for c in range(nc):
        share = (groups * clients) * weight[pl.ds(nc * j + c, 1), :] * inverse[0:1, :]
        share_ref[c] = share[0, 0]
    if groups > 1:
        for k in range(len(ends) - 1):
            final_copy(k).wait_send()


def local(updates, sample_counts):
    nc, rows, cols = updates.shape
    devices, cores = lax.axis_size("client"), lax.axis_size("param")
    groups = GROUPS if devices % GROUPS == 0 and devices > GROUPS else 1
    members = devices // groups
    tiles = cols // LANES
    bounds = sorted({tiles, *range(0, tiles, CHUNK_TILES)})
    ends = sorted({0, tiles} | {round(end * tiles) for end in LAST_ENDS})
    chunks = len(bounds) - 1
    mine = rows // devices
    if rows % devices or mine != SUBLANES or cols % LANES or members < 2 or members & (members - 1) or nc * members > LANES:
        return local_plain(updates, sample_counts)
    clients = nc * members
    f32 = jnp.float32
    dma = pltpu.SemaphoreType.DMA
    wide = cols + LANES
    return pl.pallas_call(
        functools.partial(kernel, groups, members, cores, bounds, ends),
        out_shape=(pltpu.VMEM((mine, cols), f32), pltpu.SMEM((nc,), f32)),
        in_specs=[pl.BlockSpec(memory_space=pltpu.HBM)] * 2,
        out_specs=(pl.BlockSpec(memory_space=pltpu.VMEM), pl.BlockSpec(memory_space=pltpu.SMEM)),
        scratch_shapes=[
            pltpu.VMEM((members, nc, groups, mine, cols), f32),
            pltpu.SMEM((nc,), jnp.int32),
            pltpu.VMEM((nc, LANES), f32),
            pltpu.VMEM((members, nc, LANES), f32),
            pltpu.VMEM((ITERS, 1, LANES), f32),
            pltpu.VMEM((ITERS, cores * members, 1, LANES), f32),
            pltpu.VMEM((clients, LANES), f32),
            pltpu.VMEM((clients, LANES), f32),
            pltpu.VMEM((ITERS, groups, mine, wide), f32),
            pltpu.VMEM((ITERS, groups, mine, wide), f32),
            pltpu.VMEM((mine, wide), f32),
            pltpu.VMEM((mine, wide), f32),
            dma,
            dma((chunks,)),
            dma((members, chunks)),
            dma((members, chunks)),
            dma((members,)),
            dma((members,)),
            dma((ITERS, chunks)),
            dma((ITERS, chunks)),
            dma((len(ends) - 1,)),
            dma((len(ends) - 1,)),
            dma((ITERS, cores * members)),
            dma((ITERS, cores * members)),
        ],
        compiler_params=pltpu.CompilerParams(
            collective_id=0, has_side_effects=True, vmem_limit_bytes=56 * 1024 * 1024),
        cost_estimate=pl.CostEstimate(
            flops=16 * clients * groups * mine * cols, bytes_accessed=8 * nc * rows * cols, transcendentals=0),
    )(updates.reshape(nc, groups, members, mine, cols), sample_counts)


def solution(mesh):
    return jax.shard_map(
        local,
        mesh=mesh,
        in_specs=(P("client", None, "param"), P("client")),
        out_specs=(P("client", "param"), P("client")),
        check_vma=False,
    )
```

```python
import functools

import jax
import jax.numpy as jnp
from jax import lax
from jax.experimental import pallas as pl
from jax.experimental.pallas import tpu as pltpu
from jax.sharding import PartitionSpec as P

ITERS = 2
LANES = 128
SUBLANES = 8
GROUPS = 2
CHUNK_TILES = 2
IN_FLIGHT = 3
LAST_ENDS = (0.43, 1.0)

smoothing = 1e-06


def weighted_sum(weights, updates):
    return jnp.einsum("c,crk->rk", weights, updates, precision=lax.Precision.HIGHEST)


def local_plain(updates, sample_counts):
    local_clients = updates.shape[0]
    clients = local_clients * lax.axis_size("client")
    exchanged = lax.all_to_all(updates, "client", split_axis=1, concat_axis=0, tiled=True)
    counts_f = lax.all_gather(sample_counts, "client", axis=0, tiled=True).astype(jnp.float32)
    weights = counts_f
    for iteration in range(ITERS + 1):
        weight_sum = jnp.sum(weights)
        median = weighted_sum(weights, exchanged) / weight_sum
        if iteration < ITERS:
            distance_sq = jnp.sum((exchanged - median[None]) ** 2, axis=(1, 2))
            distance_sq = lax.psum(distance_sq, ("client", "param"))
            weights = counts_f / jnp.sqrt(distance_sq + smoothing)
    offset = lax.axis_index("client") * local_clients
    shares = lax.dynamic_slice_in_dim(clients * weights / weight_sum, offset, local_clients, 0)
    return (median, shares)


def kernel(groups, members, cores, bounds, ends, u_ref, cnt_hbm, med_ref, share_ref,
           held, cnt_ref, cnt_send, cnt_held, dist_send, dist_held, dist_rows, weight, part, part_in, last, last_in, pre_u, pre, pre_in,
           in_sem, own_sem, u_send, u_recv, c_send, c_recv, p_send, p_recv, l_send, l_recv, d_send, d_recv,
           pre_sem, pre_send, pre_recv):
    nc, cols = u_ref.shape[0], u_ref.shape[-1]
    clients = nc * members
    me, core = lax.axis_index("client"), lax.axis_index("param")
    j, h = lax.rem(me, members), lax.div(me, members)
    partner = lax.rem(me + members, groups * members)
    rank = core * members + j
    chunks = len(bounds) - 1

    def lanes(k):
        return pl.ds(bounds[k] * LANES, (bounds[k + 1] - bounds[k]) * LANES)

    def member(o, c):
        return {"client": h * members + flipped(o), "param": lax.rem(core + c, cores)}

    def flipped(m):
        return sum(b * lax.rem(lax.rem(lax.div(j, b), 2) + (m // b) % 2, 2) for b in bits)

    full = members - 1
    bits = [1 << b for b in range(full.bit_length())]
    others = sorted(((o, c) for c in range(cores) for o in range(members) if o or c),
                    key=lambda x: -bin(x[0]).count("1"))
    barrier = pltpu.get_barrier_semaphore()
    for o, c in others:
        pl.semaphore_signal(barrier, inc=1, device_id=member(o, c), device_id_type=pl.DeviceIdType.MESH)
    if groups > 1:
        for m in range(members):
            pl.semaphore_signal(barrier, inc=1, device_id={"client": (1 - h) * members + flipped(m)},
                                device_id_type=pl.DeviceIdType.MESH)
    counts_in = pltpu.make_async_copy(cnt_hbm, cnt_ref, in_sem)
    counts_in.start()
    own = []
    for k in range(chunks):
        sl = lanes(k)
        own.append(pltpu.make_async_copy(u_ref.at[:, :, j, :, sl], held.at[j, :, :, :, sl], own_sem.at[k]))
        own[-1].start()
    early = pltpu.make_async_copy(u_ref.at[:, :, :, :, lanes(chunks - 1)], pre_u, pre_sem)
    if groups > 1:
        early.start()
    pl.semaphore_wait(barrier, len(others) + (members if groups > 1 else 0))

    masks = [full] + [m for low in range(members // 2 - 1, 0, -1) for m in (full - low, low)]

    def peer(o):
        m, index = masks[o - 1], 0
        for b in bits:
            flip = (m // b) % 2
            if m != full:
                flip = flip + lax.rem(core, 2) * (1 - 2 * flip)
            index = index + b * lax.rem(lax.rem(lax.div(j, b), 2) + flip, 2)
        return index

    def count_copy(o, slot):
        return pltpu.make_async_remote_copy(
            src_ref=cnt_send, dst_ref=cnt_held.at[slot], send_sem=c_send.at[o], recv_sem=c_recv.at[o],
            device_id={"client": h * members + peer(o)}, device_id_type=pl.DeviceIdType.MESH)

    def rows_copy(o, k, slot):
        to = peer(o)
        sl = lanes(k)
        return pltpu.make_async_remote_copy(
            src_ref=u_ref.at[:, :, to, :, sl], dst_ref=held.at[slot, :, :, :, sl],
            send_sem=u_send.at[o, k], recv_sem=u_recv.at[o, k],
            device_id={"client": h * members + to}, device_id_type=pl.DeviceIdType.MESH)

    for k in range(min(IN_FLIGHT, chunks)):
        for o in range(1, members):
            rows_copy(o, k, j).start()
        if k == 0:
            counts_in.wait()
            for c in range(nc):
                row = jnp.full((1, LANES), cnt_ref[c], jnp.int32).astype(jnp.float32)
                cnt_send[c:c + 1, :] = row
                cnt_held[j, c:c + 1, :] = row
            for o in range(1, members):
                count_copy(o, j).start()

    def pre_copy(m, slot):
        return pltpu.make_async_remote_copy(
            src_ref=pre.at[flipped(m)], dst_ref=pre_in.at[slot], send_sem=pre_send.at[m], recv_sem=pre_recv.at[m],
            device_id={"client": (1 - h) * members + flipped(m)}, device_id_type=pl.DeviceIdType.MESH)

    if groups > 1:
        early.wait()

        def presum(q, carry):
            for r in range(groups):
                x = cnt_send[0:1, 0:1] * pre_u[0, r, q]
                for c in range(1, nc):
                    x = x + cnt_send[c:c + 1, 0:1] * pre_u[c, r, q]
                pre[q, r] = x
            return carry

        lax.fori_loop(0, members, presum, 0)
        for m in reversed(range(members)):
            pre_copy(m, j).start()

    def part_copy(i, k):
        first = bounds[k] + (k > 0)
        sl = pl.ds(first * LANES, (bounds[k + 1] + 1 - first) * LANES)
        return pltpu.make_async_remote_copy(
            src_ref=part.at[i, :, :, sl], dst_ref=part_in.at[i, :, :, sl],
            send_sem=p_send.at[i, k], recv_sem=p_recv.at[i, k],
            device_id={"client": partner}, device_id_type=pl.DeviceIdType.MESH)

    def dist_copy(i, n, o, c, slot):
        return pltpu.make_async_remote_copy(
            src_ref=dist_send.at[i], dst_ref=dist_held.at[i, slot],
            send_sem=d_send.at[i, n], recv_sem=d_recv.at[i, n],
            device_id=member(o, c), device_id_type=pl.DeviceIdType.MESH)

    def weights_now():
        w = [jnp.broadcast_to(weight[c:c + 1, :], (SUBLANES, LANES)) for c in range(clients)]
        total = w[0]
        for x in w[1:]:
            total = total + x
        return w, total

    def tile(t):
        return pl.ds(pl.multiple_of(t * LANES, LANES), LANES)

    def after(t):
        return pl.ds(pl.multiple_of((t + 1) * LANES, LANES), LANES)

    def sum_tile(w, r, t):
        sums = []
        for c in range(clients):
            x = w[c] * held[c // nc, c % nc, r, :, tile(t)]
            if c < 4:
                sums.append(x)
            else:
                sums[c % 4] = sums[c % 4] + x
        while len(sums) > 1:
            sums = [sums[n] + sums[n + 1] if n + 1 < len(sums) else sums[n] for n in range(0, len(sums), 2)]
        return sums[0]

    def exchanged(i, k):
        return groups > 1 and not (i == 0 and 0 < k == chunks - 1)

    def iteration(i):
        w, total = weights_now()
        for r in range(groups):
            part[i, r, :, pl.ds(0, LANES)] = total

        def send_part(k):
            def body(t, carry):
                for r in range(groups):
                    part[i, r, :, after(t)] = sum_tile(w, r, t)
                return carry

            lax.fori_loop(bounds[k], bounds[k + 1], body, 0)
            if exchanged(i, k):
                part_copy(i, k).start()
            elif groups > 1:
                for m in range(members):
                    pre_copy(m, flipped(m)).wait_recv()
                for r in range(groups):
                    x = pre_in[0, r]
                    for q in range(1, members):
                        x = x + pre_in[q, r]
                    part_in[i, r, :, pl.ds((bounds[k] + 1) * LANES, (bounds[k + 1] - bounds[k]) * LANES)] = x

        def add_distances(k, inverse, acc):
            if exchanged(i, k):
                part_copy(i, k).wait_recv()
            if inverse is None:
                whole = part[i, 0, :, pl.ds(0, LANES)]
                if groups > 1:
                    whole = whole + part_in[i, 0, :, pl.ds(0, LANES)]
                inverse = 1.0 / whole

            def body(t, acc):
                acc = list(acc)
                for r in range(groups):
                    m = part[i, r, :, after(t)]
                    if groups > 1:
                        m = m + part_in[i, r, :, after(t)]
                    m = m * inverse
                    for c in range(clients):
                        d = held[c // nc, c % nc, r, :, tile(t)] - m
                        acc[c] = acc[c] + d * d
                return tuple(acc)

            return inverse, lax.fori_loop(bounds[k], bounds[k + 1], body, acc)

        inverse, acc = None, tuple(jnp.zeros((SUBLANES, LANES), jnp.float32) for _ in range(clients))
        for k in range(chunks):
            if i == 0:
                own[k].wait()
                for o in range(1, members):
                    rows_copy(o, k, peer(o)).wait_recv()
                    if k + IN_FLIGHT < chunks:
                        rows_copy(o, k + IN_FLIGHT, j).start()
            send_part(k)
            if i == 0 and k > 0:
                inverse, acc = add_distances(k - 1, inverse, acc)
        if i == 1:
            if groups > 1:
                for m in range(members):
                    pre_copy(m, j).wait_send()
            for o in range(1, members):
                count_copy(o, j).wait_send()
                for k in range(chunks):
                    rows_copy(o, k, j).wait_send()
        if i > 0:
            for n, (o, c) in enumerate(others):
                dist_copy(i - 1, n, o, c, rank).wait_send()
        for k in range(chunks - 1 if i == 0 else 0, chunks):
            inverse, acc = add_distances(k, inverse, acc)
        for c in range(clients):
            dist_rows[c:c + 1, :] = jnp.sum(acc[c], axis=0, keepdims=True)
        eye = (lax.broadcasted_iota(jnp.int32, (clients, LANES), 0)
               == lax.broadcasted_iota(jnp.int32, (clients, LANES), 1))
        column = jnp.sum(dist_rows[...], axis=1, keepdims=True)
        row = jnp.sum(jnp.where(eye, column, 0.0), axis=0, keepdims=True)
        dist_send[i] = row
        dist_held[i, rank] = row

        for n, (o, c) in enumerate(others):
            dist_copy(i, n, o, c, rank).start()
        for n, (o, c) in enumerate(others):
            dist_copy(i, n, o, c, lax.rem(core + cores - c, cores) * members + flipped(o)).wait_recv()
        row = dist_held[i, 0]
        for s in range(1, cores * members):
            row = row + dist_held[i, s]
        column = jnp.sum(jnp.where(eye, jnp.broadcast_to(row, eye.shape), 0.0), axis=1, keepdims=True)
        root = jnp.sqrt(jnp.broadcast_to(column, eye.shape) + smoothing)
        for c in range(clients):
            weight[c:c + 1, :] = cnt_held[c // nc, c % nc:c % nc + 1, :] / root[c:c + 1, :]

    for o in range(1, members):
        count_copy(o, peer(o)).wait_recv()
    for c in range(clients):
        weight[c:c + 1, :] = cnt_held[c // nc, c % nc:c % nc + 1, :]
    for i in range(ITERS):
        iteration(i)

    w, total = weights_now()
    def final_copy(k):
        first = ends[k] + (k > 0)
        sl = pl.ds(first * LANES, (ends[k + 1] + 1 - first) * LANES)
        return pltpu.make_async_remote_copy(
            src_ref=last.at[:, sl], dst_ref=last_in.at[:, sl], send_sem=l_send.at[k], recv_sem=l_recv.at[k],
            device_id={"client": partner}, device_id_type=pl.DeviceIdType.MESH)

    if groups > 1:
        last[:, pl.ds(0, LANES)] = total

        def body(t, carry):
            last[:, after(t)] = sum_tile(w, 1 - h, t)
            return carry

        for k in range(len(ends) - 1):
            lax.fori_loop(ends[k], ends[k + 1], body, 0)
            final_copy(k).start()

    def body(t, carry):
        med_ref[:, tile(t)] = sum_tile(w, h, t)
        return carry

    lax.fori_loop(0, cols // LANES, body, 0)
    for n, (o, c) in enumerate(others):
        dist_copy(ITERS - 1, n, o, c, rank).wait_send()
    if groups > 1:
        for i in range(ITERS):
            for k in range(chunks):
                if exchanged(i, k):
                    part_copy(i, k).wait_send()
        final_copy(0).wait_recv()
        total = total + last_in[:, pl.ds(0, LANES)]
    inverse = 1.0 / total

    def body(t, carry):
        m = med_ref[:, tile(t)]
        if groups > 1:
            m = m + last_in[:, after(t)]
        med_ref[:, tile(t)] = m * inverse
        return carry

    for k in range(len(ends) - 1):
        if groups > 1 and k > 0:
            final_copy(k).wait_recv()
        lax.fori_loop(ends[k], ends[k + 1], body, 0)
    for c in range(nc):
        share = (groups * clients) * weight[pl.ds(nc * j + c, 1), :] * inverse[0:1, :]
        share_ref[c] = share[0, 0]
    if groups > 1:
        for k in range(len(ends) - 1):
            final_copy(k).wait_send()


def local(updates, sample_counts):
    nc, rows, cols = updates.shape
    devices, cores = lax.axis_size("client"), lax.axis_size("param")
    groups = GROUPS if devices % GROUPS == 0 and devices > GROUPS else 1
    members = devices // groups
    tiles = cols // LANES
    bounds = sorted({tiles, *range(0, tiles, CHUNK_TILES)})
    ends = sorted({0, tiles} | {round(end * tiles) for end in LAST_ENDS})
    chunks = len(bounds) - 1
    mine = rows // devices
    if rows % devices or mine != SUBLANES or cols % LANES or members < 2 or members & (members - 1) or tiles <= CHUNK_TILES or nc * members > LANES:
        return local_plain(updates, sample_counts)
    clients = nc * members
    f32 = jnp.float32
    dma = pltpu.SemaphoreType.DMA
    wide = cols + LANES
    tail = (tiles - bounds[-2]) * LANES
    return pl.pallas_call(
        functools.partial(kernel, groups, members, cores, bounds, ends),
        out_shape=(pltpu.VMEM((mine, cols), f32), pltpu.SMEM((nc,), f32)),
        in_specs=[pl.BlockSpec(memory_space=pltpu.HBM)] * 2,
        out_specs=(pl.BlockSpec(memory_space=pltpu.VMEM), pl.BlockSpec(memory_space=pltpu.SMEM)),
        scratch_shapes=[
            pltpu.VMEM((members, nc, groups, mine, cols), f32),
            pltpu.SMEM((nc,), jnp.int32),
            pltpu.VMEM((nc, LANES), f32),
            pltpu.VMEM((members, nc, LANES), f32),
            pltpu.VMEM((ITERS, 1, LANES), f32),
            pltpu.VMEM((ITERS, cores * members, 1, LANES), f32),
            pltpu.VMEM((clients, LANES), f32),
            pltpu.VMEM((clients, LANES), f32),
            pltpu.VMEM((ITERS, groups, mine, wide), f32),
            pltpu.VMEM((ITERS, groups, mine, wide), f32),
            pltpu.VMEM((mine, wide), f32),
            pltpu.VMEM((mine, wide), f32),
            pltpu.VMEM((nc, groups, members, mine, tail), f32),
            pltpu.VMEM((members, groups, mine, tail), f32),
            pltpu.VMEM((members, groups, mine, tail), f32),
            dma,
            dma((chunks,)),
            dma((members, chunks)),
            dma((members, chunks)),
            dma((members,)),
            dma((members,)),
            dma((ITERS, chunks)),
            dma((ITERS, chunks)),
            dma((len(ends) - 1,)),
            dma((len(ends) - 1,)),
            dma((ITERS, cores * members)),
            dma((ITERS, cores * members)),
            dma,
            dma((members,)),
            dma((members,)),
        ],
        compiler_params=pltpu.CompilerParams(
            collective_id=0, has_side_effects=True, vmem_limit_bytes=56 * 1024 * 1024),
        cost_estimate=pl.CostEstimate(
            flops=16 * clients * groups * mine * cols, bytes_accessed=8 * nc * rows * cols, transcendentals=0),
    )(updates.reshape(nc, groups, members, mine, cols), sample_counts)


def solution(mesh):
    return jax.shard_map(
        local,
        mesh=mesh,
        in_specs=(P("client", None, "param"), P("client")),
        out_specs=(P("client", "param"), P("client")),
        check_vma=False,
    )
```

```python
import functools

import jax
import jax.numpy as jnp
from jax import lax
from jax.experimental import pallas as pl
from jax.experimental.pallas import tpu as pltpu
from jax.sharding import PartitionSpec as P

ITERS = 2
LANES = 128
SUBLANES = 8
GROUPS = 2
CHUNK_ENDS = (0.57, 1.0)
LAST_ENDS = (0.43, 1.0)

smoothing = 1e-06


def weighted_sum(weights, updates):
    return jnp.einsum("c,crk->rk", weights, updates, precision=lax.Precision.HIGHEST)


def local_plain(updates, sample_counts):
    local_clients = updates.shape[0]
    clients = local_clients * lax.axis_size("client")
    exchanged = lax.all_to_all(updates, "client", split_axis=1, concat_axis=0, tiled=True)
    counts_f = lax.all_gather(sample_counts, "client", axis=0, tiled=True).astype(jnp.float32)
    weights = counts_f
    for iteration in range(ITERS + 1):
        weight_sum = jnp.sum(weights)
        median = weighted_sum(weights, exchanged) / weight_sum
        if iteration < ITERS:
            distance_sq = jnp.sum((exchanged - median[None]) ** 2, axis=(1, 2))
            distance_sq = lax.psum(distance_sq, ("client", "param"))
            weights = counts_f / jnp.sqrt(distance_sq + smoothing)
    offset = lax.axis_index("client") * local_clients
    shares = lax.dynamic_slice_in_dim(clients * weights / weight_sum, offset, local_clients, 0)
    return (median, shares)


def kernel(groups, members, cores, bounds, ends, u_ref, cnt_hbm, med_ref, share_ref,
           held, cnt_ref, cnt_send, cnt_held, dist_send, dist_held, dist_rows, weight, part, part_in, last, last_in,
           in_sem, own_sem, u_send, u_recv, c_send, c_recv, p_send, p_recv, l_send, l_recv, d_send, d_recv):
    nc, cols = u_ref.shape[0], u_ref.shape[-1]
    clients = nc * members
    me, core = lax.axis_index("client"), lax.axis_index("param")
    j, h = lax.rem(me, members), lax.div(me, members)
    partner = lax.rem(me + members, groups * members)
    rank = core * members + j
    chunks = len(bounds) - 1

    def lanes(k):
        return pl.ds(bounds[k] * LANES, (bounds[k + 1] - bounds[k]) * LANES)

    bits = [1 << b for b in range((members - 1).bit_length())]

    def flipped(m):
        return sum(b * lax.rem(lax.rem(lax.div(j, b), 2) + lax.rem(lax.div(m, b), 2), 2) for b in bits)

    def member(n):
        o, c = lax.rem(n, members), lax.div(n, members)
        return {"client": h * members + flipped(o), "param": lax.rem(core + c, cores)}

    def slot_of(n):
        o, c = lax.rem(n, members), lax.div(n, members)
        return lax.rem(core + c, cores) * members + flipped(o)

    def each(low, high, do):
        def body(n, carry):
            do(n)
            return carry

        lax.fori_loop(low, high, body, 0)

    everyone = cores * members
    barrier = pltpu.get_barrier_semaphore()
    each(1, everyone, lambda n: pl.semaphore_signal(
        barrier, inc=1, device_id=member(n), device_id_type=pl.DeviceIdType.MESH))
    if groups > 1:
        pl.semaphore_signal(barrier, inc=1, device_id={"client": partner}, device_id_type=pl.DeviceIdType.MESH)
    counts_in = pltpu.make_async_copy(cnt_hbm, cnt_ref, in_sem)
    counts_in.start()
    own = []
    for k in range(chunks):
        sl = lanes(k)
        own.append(pltpu.make_async_copy(u_ref.at[:, :, j, :, sl], held.at[j, :, :, :, sl], own_sem.at[k]))
        own[-1].start()
    pl.semaphore_wait(barrier, everyone - 1 + (groups > 1))

    def peer(o):
        return flipped(o + lax.rem(core, 2) * (members - 2 * o))

    def count_copy(o, slot):
        return pltpu.make_async_remote_copy(
            src_ref=cnt_send, dst_ref=cnt_held.at[slot], send_sem=c_send.at[o], recv_sem=c_recv.at[o],
            device_id={"client": h * members + peer(o)}, device_id_type=pl.DeviceIdType.MESH)

    def rows_copy(o, k, slot):
        to = peer(o)
        sl = lanes(k)
        return pltpu.make_async_remote_copy(
            src_ref=u_ref.at[:, :, to, :, sl], dst_ref=held.at[slot, :, :, :, sl],
            send_sem=u_send.at[o, k], recv_sem=u_recv.at[o, k],
            device_id={"client": h * members + to}, device_id_type=pl.DeviceIdType.MESH)

    for k in range(chunks):
        each(1, members, lambda o, k=k: rows_copy(o, k, j).start())
        if k == 0:
            counts_in.wait()
            for c in range(nc):
                row = jnp.full((1, LANES), cnt_ref[c], jnp.int32).astype(jnp.float32)
                cnt_send[c:c + 1, :] = row
                cnt_held[j, c:c + 1, :] = row
            each(1, members, lambda o: count_copy(o, j).start())

    def part_copy(i, k):
        first = bounds[k] + (k > 0)
        sl = pl.ds(first * LANES, (bounds[k + 1] + 1 - first) * LANES)
        return pltpu.make_async_remote_copy(
            src_ref=part.at[i, :, :, sl], dst_ref=part_in.at[i, :, :, sl],
            send_sem=p_send.at[i, k], recv_sem=p_recv.at[i, k],
            device_id={"client": partner}, device_id_type=pl.DeviceIdType.MESH)

    def dist_copy(i, n, slot):
        return pltpu.make_async_remote_copy(
            src_ref=dist_send.at[i], dst_ref=dist_held.at[i, slot],
            send_sem=d_send.at[i, n], recv_sem=d_recv.at[i, n],
            device_id=member(n), device_id_type=pl.DeviceIdType.MESH)

    def weights_now():
        w = [jnp.broadcast_to(weight[c:c + 1, :], (SUBLANES, LANES)) for c in range(clients)]
        total = w[0]
        for x in w[1:]:
            total = total + x
        return w, total

    def tile(t):
        return pl.ds(pl.multiple_of(t * LANES, LANES), LANES)

    def after(t):
        return pl.ds(pl.multiple_of((t + 1) * LANES, LANES), LANES)

    def sum_tile(w, r, t):
        sums = []
        for c in range(clients):
            x = w[c] * held[c // nc, c % nc, r, :, tile(t)]
            if c < 4:
                sums.append(x)
            else:
                sums[c % 4] = sums[c % 4] + x
        while len(sums) > 1:
            sums = [sums[n] + sums[n + 1] if n + 1 < len(sums) else sums[n] for n in range(0, len(sums), 2)]
        return sums[0]

    def iteration(i):
        w, total = weights_now()
        for r in range(groups):
            part[i, r, :, pl.ds(0, LANES)] = total

        def send_part(k):
            def body(t, carry):
                for r in range(groups):
                    part[i, r, :, after(t)] = sum_tile(w, r, t)
                return carry

            lax.fori_loop(bounds[k], bounds[k + 1], body, 0)
            if groups > 1:
                part_copy(i, k).start()

        def add_distances(k, inverse, acc):
            if groups > 1:
                part_copy(i, k).wait_recv()
            if inverse is None:
                whole = part[i, 0, :, pl.ds(0, LANES)]
                if groups > 1:
                    whole = whole + part_in[i, 0, :, pl.ds(0, LANES)]
                inverse = 1.0 / whole

            def body(t, acc):
                acc = list(acc)
                for r in range(groups):
                    m = part[i, r, :, after(t)]
                    if groups > 1:
                        m = m + part_in[i, r, :, after(t)]
                    m = m * inverse
                    for c in range(clients):
                        d = held[c // nc, c % nc, r, :, tile(t)] - m
                        acc[c] = acc[c] + d * d
                return tuple(acc)

            return inverse, lax.fori_loop(bounds[k], bounds[k + 1], body, acc)

        for k in range(chunks):
            @pl.when(i == 0)
            def _(k=k):
                own[k].wait()
                each(1, members, lambda o: rows_copy(o, k, peer(o)).wait_recv())

            send_part(k)

        @pl.when(i == 1)
        def _():
            def sent(o):
                count_copy(o, j).wait_send()
                for k in range(chunks):
                    rows_copy(o, k, j).wait_send()

            each(1, members, sent)

        inverse, acc = None, tuple(jnp.zeros((SUBLANES, LANES), jnp.float32) for _ in range(clients))
        for k in range(chunks):
            inverse, acc = add_distances(k, inverse, acc)
        for c in range(clients):
            dist_rows[c:c + 1, :] = jnp.sum(acc[c], axis=0, keepdims=True)
        eye = (lax.broadcasted_iota(jnp.int32, (clients, LANES), 0)
               == lax.broadcasted_iota(jnp.int32, (clients, LANES), 1))
        column = jnp.sum(dist_rows[...], axis=1, keepdims=True)
        row = jnp.sum(jnp.where(eye, column, 0.0), axis=0, keepdims=True)
        dist_send[i] = row
        dist_held[i, rank] = row

        each(1, everyone, lambda n: dist_copy(i, n, rank).start())
        each(1, everyone, lambda n: dist_copy(i, n, slot_of(n)).wait_recv())
        row = dist_held[i, 0]
        for s in range(1, cores * members):
            row = row + dist_held[i, s]
        column = jnp.sum(jnp.where(eye, jnp.broadcast_to(row, eye.shape), 0.0), axis=1, keepdims=True)
        root = jnp.sqrt(jnp.broadcast_to(column, eye.shape) + smoothing)
        for c in range(clients):
            weight[c:c + 1, :] = cnt_held[c // nc, c % nc:c % nc + 1, :] / root[c:c + 1, :]

    each(1, members, lambda o: count_copy(o, peer(o)).wait_recv())
    for c in range(clients):
        weight[c:c + 1, :] = cnt_held[c // nc, c % nc:c % nc + 1, :]
    each(0, ITERS, iteration)

    w, total = weights_now()
    def final_copy(k):
        first = ends[k] + (k > 0)
        sl = pl.ds(first * LANES, (ends[k + 1] + 1 - first) * LANES)
        return pltpu.make_async_remote_copy(
            src_ref=last.at[:, sl], dst_ref=last_in.at[:, sl], send_sem=l_send.at[k], recv_sem=l_recv.at[k],
            device_id={"client": partner}, device_id_type=pl.DeviceIdType.MESH)

    if groups > 1:
        last[:, pl.ds(0, LANES)] = total

        def body(t, carry):
            last[:, after(t)] = sum_tile(w, 1 - h, t)
            return carry

        for k in range(len(ends) - 1):
            lax.fori_loop(ends[k], ends[k + 1], body, 0)
            final_copy(k).start()

    def body(t, carry):
        med_ref[:, tile(t)] = sum_tile(w, h, t)
        return carry

    lax.fori_loop(0, cols // LANES, body, 0)
    each(1, everyone, lambda n: [dist_copy(i, n, rank).wait_send() for i in range(ITERS)])
    if groups > 1:
        for i in range(ITERS):
            for k in range(chunks):
                part_copy(i, k).wait_send()
        final_copy(0).wait_recv()
        total = total + last_in[:, pl.ds(0, LANES)]
    inverse = 1.0 / total

    def body(t, carry):
        m = med_ref[:, tile(t)]
        if groups > 1:
            m = m + last_in[:, after(t)]
        med_ref[:, tile(t)] = m * inverse
        return carry

    for k in range(len(ends) - 1):
        if groups > 1 and k > 0:
            final_copy(k).wait_recv()
        lax.fori_loop(ends[k], ends[k + 1], body, 0)
    for c in range(nc):
        share = (groups * clients) * weight[pl.ds(nc * j + c, 1), :] * inverse[0:1, :]
        share_ref[c] = share[0, 0]
    if groups > 1:
        for k in range(len(ends) - 1):
            final_copy(k).wait_send()


def local(updates, sample_counts):
    nc, rows, cols = updates.shape
    devices, cores = lax.axis_size("client"), lax.axis_size("param")
    groups = GROUPS if devices % GROUPS == 0 and devices > GROUPS else 1
    members = devices // groups
    tiles = cols // LANES
    bounds = sorted({0, tiles} | {round(end * tiles) for end in CHUNK_ENDS})
    ends = sorted({0, tiles} | {round(end * tiles) for end in LAST_ENDS})
    chunks = len(bounds) - 1
    mine = rows // devices
    if rows % devices or mine != SUBLANES or cols % LANES or members < 2 or members & (members - 1) or nc * members > LANES:
        return local_plain(updates, sample_counts)
    clients = nc * members
    f32 = jnp.float32
    dma = pltpu.SemaphoreType.DMA
    wide = cols + LANES
    return pl.pallas_call(
        functools.partial(kernel, groups, members, cores, bounds, ends),
        out_shape=(pltpu.VMEM((mine, cols), f32), pltpu.SMEM((nc,), f32)),
        in_specs=[pl.BlockSpec(memory_space=pltpu.HBM)] * 2,
        out_specs=(pl.BlockSpec(memory_space=pltpu.VMEM), pl.BlockSpec(memory_space=pltpu.SMEM)),
        scratch_shapes=[
            pltpu.VMEM((members, nc, groups, mine, cols), f32),
            pltpu.SMEM((nc,), jnp.int32),
            pltpu.VMEM((nc, LANES), f32),
            pltpu.VMEM((members, nc, LANES), f32),
            pltpu.VMEM((ITERS, 1, LANES), f32),
            pltpu.VMEM((ITERS, cores * members, 1, LANES), f32),
            pltpu.VMEM((clients, LANES), f32),
            pltpu.VMEM((clients, LANES), f32),
            pltpu.VMEM((ITERS, groups, mine, wide), f32),
            pltpu.VMEM((ITERS, groups, mine, wide), f32),
            pltpu.VMEM((mine, wide), f32),
            pltpu.VMEM((mine, wide), f32),
            dma,
            dma((chunks,)),
            dma((members, chunks)),
            dma((members, chunks)),
            dma((members,)),
            dma((members,)),
            dma((ITERS, chunks)),
            dma((ITERS, chunks)),
            dma((len(ends) - 1,)),
            dma((len(ends) - 1,)),
            dma((ITERS, cores * members)),
            dma((ITERS, cores * members)),
        ],
        compiler_params=pltpu.CompilerParams(
            collective_id=0, has_side_effects=True, vmem_limit_bytes=56 * 1024 * 1024),
        cost_estimate=pl.CostEstimate(
            flops=16 * clients * groups * mine * cols, bytes_accessed=8 * nc * rows * cols, transcendentals=0),
    )(updates.reshape(nc, groups, members, mine, cols), sample_counts)


def solution(mesh):
    return jax.shard_map(
        local,
        mesh=mesh,
        in_specs=(P("client", None, "param"), P("client")),
        out_specs=(P("client", "param"), P("client")),
        check_vma=False,
    )
```

```python
import functools

import jax
import jax.numpy as jnp
from jax import lax
from jax.experimental import pallas as pl
from jax.experimental.pallas import tpu as pltpu
from jax.sharding import PartitionSpec as P

ITERS = 2
LANES = 128
SUBLANES = 8
GROUPS = 2
CHUNK_ENDS = (0.57, 1.0)
IN_FLIGHT = 2
LAST_ENDS = (0.43, 1.0)

smoothing = 1e-06


def weighted_sum(weights, updates):
    return jnp.einsum("c,crk->rk", weights, updates, precision=lax.Precision.HIGHEST)


def local_plain(updates, sample_counts):
    local_clients = updates.shape[0]
    clients = local_clients * lax.axis_size("client")
    exchanged = lax.all_to_all(updates, "client", split_axis=1, concat_axis=0, tiled=True)
    counts_f = lax.all_gather(sample_counts, "client", axis=0, tiled=True).astype(jnp.float32)
    weights = counts_f
    for iteration in range(ITERS + 1):
        weight_sum = jnp.sum(weights)
        median = weighted_sum(weights, exchanged) / weight_sum
        if iteration < ITERS:
            distance_sq = jnp.sum((exchanged - median[None]) ** 2, axis=(1, 2))
            distance_sq = lax.psum(distance_sq, ("client", "param"))
            weights = counts_f / jnp.sqrt(distance_sq + smoothing)
    offset = lax.axis_index("client") * local_clients
    shares = lax.dynamic_slice_in_dim(clients * weights / weight_sum, offset, local_clients, 0)
    return (median, shares)


def kernel(groups, members, cores, bounds, ends, u_ref, cnt_hbm, med_ref, share_ref,
           held, cnt_ref, cnt_send, cnt_held, dist_send, dist_held, dist_rows, weight, part, part_in, last, last_in,
           in_sem, own_sem, u_send, u_recv, c_send, c_recv, p_send, p_recv, l_send, l_recv, d_send, d_recv):
    nc, cols = u_ref.shape[0], u_ref.shape[-1]
    clients = nc * members
    me, core = lax.axis_index("client"), lax.axis_index("param")
    j, h = lax.rem(me, members), lax.div(me, members)
    partner = lax.rem(me + members, groups * members)
    rank = core * members + j
    chunks = len(bounds) - 1

    def lanes(k):
        return pl.ds(bounds[k] * LANES, (bounds[k + 1] - bounds[k]) * LANES)

    def member(o, c):
        return {"client": h * members + flipped(o), "param": lax.rem(core + c, cores)}

    def flipped(m):
        return sum(b * lax.rem(lax.rem(lax.div(j, b), 2) + (m // b) % 2, 2) for b in bits)

    full = members - 1
    bits = [1 << b for b in range(full.bit_length())]
    others = sorted(((o, c) for c in range(cores) for o in range(members) if o or c),
                    key=lambda x: -bin(x[0]).count("1"))
    barrier = pltpu.get_barrier_semaphore()
    for o, c in others:
        pl.semaphore_signal(barrier, inc=1, device_id=member(o, c), device_id_type=pl.DeviceIdType.MESH)
    if groups > 1:
        pl.semaphore_signal(barrier, inc=1, device_id={"client": partner}, device_id_type=pl.DeviceIdType.MESH)
    counts_in = pltpu.make_async_copy(cnt_hbm, cnt_ref, in_sem)
    counts_in.start()
    own = []
    for k in range(chunks):
        sl = lanes(k)
        own.append(pltpu.make_async_copy(u_ref.at[:, :, j, :, sl], held.at[j, :, :, :, sl], own_sem.at[k]))
        own[-1].start()
    pl.semaphore_wait(barrier, len(others) + (groups > 1))

    masks = [m for low in range(1, members // 2) for m in (low, full - low)] + [full]

    def peer(o):
        m, index = masks[o - 1], 0
        for b in bits:
            flip = (m // b) % 2
            if m != full:
                flip = flip + lax.rem(core, 2) * (1 - 2 * flip)
            index = index + b * lax.rem(lax.rem(lax.div(j, b), 2) + flip, 2)
        return index

    def count_copy(o, slot):
        return pltpu.make_async_remote_copy(
            src_ref=cnt_send, dst_ref=cnt_held.at[slot], send_sem=c_send.at[o], recv_sem=c_recv.at[o],
            device_id={"client": h * members + peer(o)}, device_id_type=pl.DeviceIdType.MESH)

    def rows_copy(o, k, slot):
        to = peer(o)
        sl = lanes(k)
        return pltpu.make_async_remote_copy(
            src_ref=u_ref.at[:, :, to, :, sl], dst_ref=held.at[slot, :, :, :, sl],
            send_sem=u_send.at[o, k], recv_sem=u_recv.at[o, k],
            device_id={"client": h * members + to}, device_id_type=pl.DeviceIdType.MESH)

    sends = [(o, k) for k in range(chunks) for o in range(1, members)]
    for n, (o, k) in enumerate(sends):
        if n >= IN_FLIGHT:
            before = sends[n - IN_FLIGHT]
            rows_copy(*before, j).wait_send()
        rows_copy(o, k, j).start()
        if n == IN_FLIGHT - 1:
            counts_in.wait()
            for c in range(nc):
                row = jnp.full((1, LANES), cnt_ref[c], jnp.int32).astype(jnp.float32)
                cnt_send[c:c + 1, :] = row
                cnt_held[j, c:c + 1, :] = row
            for m in range(1, members):
                count_copy(m, j).start()

    def part_copy(i, k):
        first = bounds[k] + (k > 0)
        sl = pl.ds(first * LANES, (bounds[k + 1] + 1 - first) * LANES)
        return pltpu.make_async_remote_copy(
            src_ref=part.at[i, :, :, sl], dst_ref=part_in.at[i, :, :, sl],
            send_sem=p_send.at[i, k], recv_sem=p_recv.at[i, k],
            device_id={"client": partner}, device_id_type=pl.DeviceIdType.MESH)

    def dist_copy(i, n, o, c, slot):
        return pltpu.make_async_remote_copy(
            src_ref=dist_send.at[i], dst_ref=dist_held.at[i, slot],
            send_sem=d_send.at[i, n], recv_sem=d_recv.at[i, n],
            device_id=member(o, c), device_id_type=pl.DeviceIdType.MESH)

    def weights_now():
        w = [jnp.broadcast_to(weight[c:c + 1, :], (SUBLANES, LANES)) for c in range(clients)]
        total = w[0]
        for x in w[1:]:
            total = total + x
        return w, total

    def tile(t):
        return pl.ds(pl.multiple_of(t * LANES, LANES), LANES)

    def after(t):
        return pl.ds(pl.multiple_of((t + 1) * LANES, LANES), LANES)

    def sum_tile(w, r, t):
        sums = []
        for c in range(clients):
            x = w[c] * held[c // nc, c % nc, r, :, tile(t)]
            if c < 4:
                sums.append(x)
            else:
                sums[c % 4] = sums[c % 4] + x
        while len(sums) > 1:
            sums = [sums[n] + sums[n + 1] if n + 1 < len(sums) else sums[n] for n in range(0, len(sums), 2)]
        return sums[0]

    def iteration(i):
        w, total = weights_now()
        for r in range(groups):
            part[i, r, :, pl.ds(0, LANES)] = total

        def send_part(k):
            def body(t, carry):
                for r in range(groups):
                    part[i, r, :, after(t)] = sum_tile(w, r, t)
                return carry

            lax.fori_loop(bounds[k], bounds[k + 1], body, 0)
            if groups > 1:
                part_copy(i, k).start()

        def add_distances(k, inverse, acc):
            if groups > 1:
                part_copy(i, k).wait_recv()
            if inverse is None:
                whole = part[i, 0, :, pl.ds(0, LANES)]
                if groups > 1:
                    whole = whole + part_in[i, 0, :, pl.ds(0, LANES)]
                inverse = 1.0 / whole

            def body(t, acc):
                acc = list(acc)
                for r in range(groups):
                    m = part[i, r, :, after(t)]
                    if groups > 1:
                        m = m + part_in[i, r, :, after(t)]
                    m = m * inverse
                    for c in range(clients):
                        d = held[c // nc, c % nc, r, :, tile(t)] - m
                        acc[c] = acc[c] + d * d
                return tuple(acc)

            return inverse, lax.fori_loop(bounds[k], bounds[k + 1], body, acc)

        inverse, acc = None, tuple(jnp.zeros((SUBLANES, LANES), jnp.float32) for _ in range(clients))
        for k in range(chunks):
            if i == 0:
                own[k].wait()
                for o in range(1, members):
                    rows_copy(o, k, peer(o)).wait_recv()
            send_part(k)
            if i == 0 and k > 0:
                inverse, acc = add_distances(k - 1, inverse, acc)
        if i == 1:
            for o in range(1, members):
                count_copy(o, j).wait_send()
            for o, k in sends[-IN_FLIGHT:]:
                rows_copy(o, k, j).wait_send()
        if i > 0:
            for n, (o, c) in enumerate(others):
                dist_copy(i - 1, n, o, c, rank).wait_send()
        for k in range(chunks - 1 if i == 0 else 0, chunks):
            inverse, acc = add_distances(k, inverse, acc)
        for c in range(clients):
            dist_rows[c:c + 1, :] = jnp.sum(acc[c], axis=0, keepdims=True)
        eye = (lax.broadcasted_iota(jnp.int32, (clients, LANES), 0)
               == lax.broadcasted_iota(jnp.int32, (clients, LANES), 1))
        column = jnp.sum(dist_rows[...], axis=1, keepdims=True)
        row = jnp.sum(jnp.where(eye, column, 0.0), axis=0, keepdims=True)
        dist_send[i] = row
        dist_held[i, rank] = row

        for n, (o, c) in enumerate(others):
            dist_copy(i, n, o, c, rank).start()
        for n, (o, c) in enumerate(others):
            dist_copy(i, n, o, c, lax.rem(core + cores - c, cores) * members + flipped(o)).wait_recv()
        row = dist_held[i, 0]
        for s in range(1, cores * members):
            row = row + dist_held[i, s]
        column = jnp.sum(jnp.where(eye, jnp.broadcast_to(row, eye.shape), 0.0), axis=1, keepdims=True)
        root = jnp.sqrt(jnp.broadcast_to(column, eye.shape) + smoothing)
        for c in range(clients):
            weight[c:c + 1, :] = cnt_held[c // nc, c % nc:c % nc + 1, :] / root[c:c + 1, :]

    for o in range(1, members):
        count_copy(o, peer(o)).wait_recv()
    for c in range(clients):
        weight[c:c + 1, :] = cnt_held[c // nc, c % nc:c % nc + 1, :]
    for i in range(ITERS):
        iteration(i)

    w, total = weights_now()
    def final_copy(k):
        first = ends[k] + (k > 0)
        sl = pl.ds(first * LANES, (ends[k + 1] + 1 - first) * LANES)
        return pltpu.make_async_remote_copy(
            src_ref=last.at[:, sl], dst_ref=last_in.at[:, sl], send_sem=l_send.at[k], recv_sem=l_recv.at[k],
            device_id={"client": partner}, device_id_type=pl.DeviceIdType.MESH)

    if groups > 1:
        last[:, pl.ds(0, LANES)] = total

        def body(t, carry):
            last[:, after(t)] = sum_tile(w, 1 - h, t)
            return carry

        for k in range(len(ends) - 1):
            lax.fori_loop(ends[k], ends[k + 1], body, 0)
            final_copy(k).start()

    def body(t, carry):
        med_ref[:, tile(t)] = sum_tile(w, h, t)
        return carry

    lax.fori_loop(0, cols // LANES, body, 0)
    for n, (o, c) in enumerate(others):
        dist_copy(ITERS - 1, n, o, c, rank).wait_send()
    if groups > 1:
        for i in range(ITERS):
            for k in range(chunks):
                part_copy(i, k).wait_send()
        final_copy(0).wait_recv()
        total = total + last_in[:, pl.ds(0, LANES)]
    inverse = 1.0 / total

    def body(t, carry):
        m = med_ref[:, tile(t)]
        if groups > 1:
            m = m + last_in[:, after(t)]
        med_ref[:, tile(t)] = m * inverse
        return carry

    for k in range(len(ends) - 1):
        if groups > 1 and k > 0:
            final_copy(k).wait_recv()
        lax.fori_loop(ends[k], ends[k + 1], body, 0)
    for c in range(nc):
        share = (groups * clients) * weight[pl.ds(nc * j + c, 1), :] * inverse[0:1, :]
        share_ref[c] = share[0, 0]
    if groups > 1:
        for k in range(len(ends) - 1):
            final_copy(k).wait_send()


def local(updates, sample_counts):
    nc, rows, cols = updates.shape
    devices, cores = lax.axis_size("client"), lax.axis_size("param")
    groups = GROUPS if devices % GROUPS == 0 and devices > GROUPS else 1
    members = devices // groups
    tiles = cols // LANES
    bounds = sorted({0, tiles} | {round(end * tiles) for end in CHUNK_ENDS})
    ends = sorted({0, tiles} | {round(end * tiles) for end in LAST_ENDS})
    chunks = len(bounds) - 1
    mine = rows // devices
    if rows % devices or mine != SUBLANES or cols % LANES or members < 2 or members & (members - 1) or nc * members > LANES:
        return local_plain(updates, sample_counts)
    clients = nc * members
    f32 = jnp.float32
    dma = pltpu.SemaphoreType.DMA
    wide = cols + LANES
    return pl.pallas_call(
        functools.partial(kernel, groups, members, cores, bounds, ends),
        out_shape=(pltpu.VMEM((mine, cols), f32), pltpu.SMEM((nc,), f32)),
        in_specs=[pl.BlockSpec(memory_space=pltpu.HBM)] * 2,
        out_specs=(pl.BlockSpec(memory_space=pltpu.VMEM), pl.BlockSpec(memory_space=pltpu.SMEM)),
        scratch_shapes=[
            pltpu.VMEM((members, nc, groups, mine, cols), f32),
            pltpu.SMEM((nc,), jnp.int32),
            pltpu.VMEM((nc, LANES), f32),
            pltpu.VMEM((members, nc, LANES), f32),
            pltpu.VMEM((ITERS, 1, LANES), f32),
            pltpu.VMEM((ITERS, cores * members, 1, LANES), f32),
            pltpu.VMEM((clients, LANES), f32),
            pltpu.VMEM((clients, LANES), f32),
            pltpu.VMEM((ITERS, groups, mine, wide), f32),
            pltpu.VMEM((ITERS, groups, mine, wide), f32),
            pltpu.VMEM((mine, wide), f32),
            pltpu.VMEM((mine, wide), f32),
            dma,
            dma((chunks,)),
            dma((members, chunks)),
            dma((members, chunks)),
            dma((members,)),
            dma((members,)),
            dma((ITERS, chunks)),
            dma((ITERS, chunks)),
            dma((len(ends) - 1,)),
            dma((len(ends) - 1,)),
            dma((ITERS, cores * members)),
            dma((ITERS, cores * members)),
        ],
        compiler_params=pltpu.CompilerParams(
            collective_id=0, has_side_effects=True, vmem_limit_bytes=56 * 1024 * 1024),
        cost_estimate=pl.CostEstimate(
            flops=16 * clients * groups * mine * cols, bytes_accessed=8 * nc * rows * cols, transcendentals=0),
    )(updates.reshape(nc, groups, members, mine, cols), sample_counts)


def solution(mesh):
    return jax.shard_map(
        local,
        mesh=mesh,
        in_specs=(P("client", None, "param"), P("client")),
        out_specs=(P("client", "param"), P("client")),
        check_vma=False,
    )
```

```python
import functools

import jax
import jax.numpy as jnp
from jax import lax
from jax.experimental import pallas as pl
from jax.experimental.pallas import tpu as pltpu
from jax.sharding import PartitionSpec as P

ITERS = 2
LANES = 128
SUBLANES = 8
GROUPS = 2
CHUNK_ENDS = (0.5, 0.79, 0.93, 1.0)
LAST_ENDS = (0.43, 1.0)

smoothing = 1e-06


def weighted_sum(weights, updates):
    return jnp.einsum("c,crk->rk", weights, updates, precision=lax.Precision.HIGHEST)


def local_plain(updates, sample_counts):
    local_clients = updates.shape[0]
    clients = local_clients * lax.axis_size("client")
    exchanged = lax.all_to_all(updates, "client", split_axis=1, concat_axis=0, tiled=True)
    counts_f = lax.all_gather(sample_counts, "client", axis=0, tiled=True).astype(jnp.float32)
    weights = counts_f
    for iteration in range(ITERS + 1):
        weight_sum = jnp.sum(weights)
        median = weighted_sum(weights, exchanged) / weight_sum
        if iteration < ITERS:
            distance_sq = jnp.sum((exchanged - median[None]) ** 2, axis=(1, 2))
            distance_sq = lax.psum(distance_sq, ("client", "param"))
            weights = counts_f / jnp.sqrt(distance_sq + smoothing)
    offset = lax.axis_index("client") * local_clients
    shares = lax.dynamic_slice_in_dim(clients * weights / weight_sum, offset, local_clients, 0)
    return (median, shares)


def kernel(groups, members, cores, bounds, ends, u_ref, cnt_hbm, med_ref, share_ref,
           held, cnt_ref, cnt_send, cnt_held, dist_send, dist_held, dist_rows, weight, part, part_in, last, last_in,
           in_sem, own_sem, u_send, u_recv, c_send, c_recv, p_send, p_recv, l_send, l_recv, d_send, d_recv):
    nc, cols = u_ref.shape[0], u_ref.shape[-1]
    clients = nc * members
    me, core = lax.axis_index("client"), lax.axis_index("param")
    j, h = lax.rem(me, members), lax.div(me, members)
    partner = lax.rem(me + members, groups * members)
    rank = core * members + j
    chunks = len(bounds) - 1

    def lanes(k):
        return pl.ds(bounds[k] * LANES, (bounds[k + 1] - bounds[k]) * LANES)

    def member(o, c):
        return {"client": h * members + flipped(o), "param": lax.rem(core + c, cores)}

    def flipped(m):
        return sum(b * lax.rem(lax.rem(lax.div(j, b), 2) + (m // b) % 2, 2) for b in bits)

    full = members - 1
    bits = [1 << b for b in range(full.bit_length())]
    others = sorted(((o, c) for c in range(cores) for o in range(members) if o or c),
                    key=lambda x: -bin(x[0]).count("1"))
    barrier = pltpu.get_barrier_semaphore()
    for o, c in others:
        pl.semaphore_signal(barrier, inc=1, device_id=member(o, c), device_id_type=pl.DeviceIdType.MESH)
    if groups > 1:
        pl.semaphore_signal(barrier, inc=1, device_id={"client": partner}, device_id_type=pl.DeviceIdType.MESH)
    counts_in = pltpu.make_async_copy(cnt_hbm, cnt_ref, in_sem)
    counts_in.start()
    own = []
    for k in range(chunks):
        sl = lanes(k)
        own.append(pltpu.make_async_copy(u_ref.at[:, :, j, :, sl], held.at[j, :, :, :, sl], own_sem.at[k]))
        own[-1].start()
    pl.semaphore_wait(barrier, len(others) + (groups > 1))

    masks = [full] + [m for low in range(members // 2 - 1, 0, -1) for m in (full - low, low)]

    def peer(o):
        m, index = masks[o - 1], 0
        for b in bits:
            flip = (m // b) % 2
            if m != full:
                flip = flip + lax.rem(core, 2) * (1 - 2 * flip)
            index = index + b * lax.rem(lax.rem(lax.div(j, b), 2) + flip, 2)
        return index

    def count_copy(o, slot):
        return pltpu.make_async_remote_copy(
            src_ref=cnt_send, dst_ref=cnt_held.at[slot], send_sem=c_send.at[o], recv_sem=c_recv.at[o],
            device_id={"client": h * members + peer(o)}, device_id_type=pl.DeviceIdType.MESH)

    def rows_copy(o, k, slot):
        to = peer(o)
        sl = lanes(k)
        return pltpu.make_async_remote_copy(
            src_ref=u_ref.at[:, :, to, :, sl], dst_ref=held.at[slot, :, :, :, sl],
            send_sem=u_send.at[o, k], recv_sem=u_recv.at[o, k],
            device_id={"client": h * members + to}, device_id_type=pl.DeviceIdType.MESH)

    for k in range(chunks):
        for o in range(1, members):
            rows_copy(o, k, j).start()
        if k == 0:
            counts_in.wait()
            for c in range(nc):
                row = jnp.full((1, LANES), cnt_ref[c], jnp.int32).astype(jnp.float32)
                cnt_send[c:c + 1, :] = row
                cnt_held[j, c:c + 1, :] = row
            for o in range(1, members):
                count_copy(o, j).start()

    def part_copy(i, k):
        first = bounds[k] + (k > 0)
        sl = pl.ds(first * LANES, (bounds[k + 1] + 1 - first) * LANES)
        return pltpu.make_async_remote_copy(
            src_ref=part.at[i, :, :, sl], dst_ref=part_in.at[i, :, :, sl],
            send_sem=p_send.at[i, k], recv_sem=p_recv.at[i, k],
            device_id={"client": partner}, device_id_type=pl.DeviceIdType.MESH)

    def dist_copy(i, n, o, c, slot):
        return pltpu.make_async_remote_copy(
            src_ref=dist_send.at[i], dst_ref=dist_held.at[i, slot],
            send_sem=d_send.at[i, n], recv_sem=d_recv.at[i, n],
            device_id=member(o, c), device_id_type=pl.DeviceIdType.MESH)

    def weights_now():
        w = [jnp.broadcast_to(weight[c:c + 1, :], (SUBLANES, LANES)) for c in range(clients)]
        total = w[0]
        for x in w[1:]:
            total = total + x
        return w, total

    def tile(t):
        return pl.ds(pl.multiple_of(t * LANES, LANES), LANES)

    def after(t):
        return pl.ds(pl.multiple_of((t + 1) * LANES, LANES), LANES)

    def sum_tile(w, r, t):
        sums = []
        for c in range(clients):
            x = w[c] * held[c // nc, c % nc, r, :, tile(t)]
            if c < 4:
                sums.append(x)
            else:
                sums[c % 4] = sums[c % 4] + x
        while len(sums) > 1:
            sums = [sums[n] + sums[n + 1] if n + 1 < len(sums) else sums[n] for n in range(0, len(sums), 2)]
        return sums[0]

    def iteration(i):
        w, total = weights_now()
        for r in range(groups):
            part[i, r, :, pl.ds(0, LANES)] = total

        def send_part(k):
            def body(t, carry):
                for r in range(groups):
                    part[i, r, :, after(t)] = sum_tile(w, r, t)
                return carry

            lax.fori_loop(bounds[k], bounds[k + 1], body, 0, unroll=True)
            if groups > 1:
                part_copy(i, k).start()

        def add_distances(k, inverse, acc):
            if groups > 1:
                part_copy(i, k).wait_recv()
            if inverse is None:
                whole = part[i, 0, :, pl.ds(0, LANES)]
                if groups > 1:
                    whole = whole + part_in[i, 0, :, pl.ds(0, LANES)]
                inverse = 1.0 / whole

            def body(t, acc):
                acc = list(acc)
                for r in range(groups):
                    m = part[i, r, :, after(t)]
                    if groups > 1:
                        m = m + part_in[i, r, :, after(t)]
                    m = m * inverse
                    for c in range(clients):
                        d = held[c // nc, c % nc, r, :, tile(t)] - m
                        acc[c] = acc[c] + d * d
                return tuple(acc)

            return inverse, lax.fori_loop(bounds[k], bounds[k + 1], body, acc, unroll=True)

        inverse, acc = None, tuple(jnp.zeros((SUBLANES, LANES), jnp.float32) for _ in range(clients))
        for k in range(chunks):
            if i == 0:
                own[k].wait()
                for o in range(1, members):
                    rows_copy(o, k, peer(o)).wait_recv()
            send_part(k)
            if i == 0 and k > 0:
                inverse, acc = add_distances(k - 1, inverse, acc)
        if i == 1:
            for o in range(1, members):
                count_copy(o, j).wait_send()
                for k in range(chunks):
                    rows_copy(o, k, j).wait_send()
        if i > 0:
            for n, (o, c) in enumerate(others):
                dist_copy(i - 1, n, o, c, rank).wait_send()
        for k in range(chunks - 1 if i == 0 else 0, chunks):
            inverse, acc = add_distances(k, inverse, acc)
        for c in range(clients):
            dist_rows[c:c + 1, :] = jnp.sum(acc[c], axis=0, keepdims=True)
        eye = (lax.broadcasted_iota(jnp.int32, (clients, LANES), 0)
               == lax.broadcasted_iota(jnp.int32, (clients, LANES), 1))
        column = jnp.sum(dist_rows[...], axis=1, keepdims=True)
        row = jnp.sum(jnp.where(eye, column, 0.0), axis=0, keepdims=True)
        dist_send[i] = row
        dist_held[i, rank] = row

        for n, (o, c) in enumerate(others):
            dist_copy(i, n, o, c, rank).start()
        for n, (o, c) in enumerate(others):
            dist_copy(i, n, o, c, lax.rem(core + cores - c, cores) * members + flipped(o)).wait_recv()
        row = dist_held[i, 0]
        for s in range(1, cores * members):
            row = row + dist_held[i, s]
        column = jnp.sum(jnp.where(eye, jnp.broadcast_to(row, eye.shape), 0.0), axis=1, keepdims=True)
        root = jnp.sqrt(jnp.broadcast_to(column, eye.shape) + smoothing)
        for c in range(clients):
            weight[c:c + 1, :] = cnt_held[c // nc, c % nc:c % nc + 1, :] / root[c:c + 1, :]

    for o in range(1, members):
        count_copy(o, peer(o)).wait_recv()
    for c in range(clients):
        weight[c:c + 1, :] = cnt_held[c // nc, c % nc:c % nc + 1, :]
    for i in range(ITERS):
        iteration(i)

    w, total = weights_now()
    def final_copy(k):
        first = ends[k] + (k > 0)
        sl = pl.ds(first * LANES, (ends[k + 1] + 1 - first) * LANES)
        return pltpu.make_async_remote_copy(
            src_ref=last.at[:, sl], dst_ref=last_in.at[:, sl], send_sem=l_send.at[k], recv_sem=l_recv.at[k],
            device_id={"client": partner}, device_id_type=pl.DeviceIdType.MESH)

    if groups > 1:
        last[:, pl.ds(0, LANES)] = total

        def body(t, carry):
            last[:, after(t)] = sum_tile(w, 1 - h, t)
            return carry

        for k in range(len(ends) - 1):
            lax.fori_loop(ends[k], ends[k + 1], body, 0, unroll=True)
            final_copy(k).start()

    def body(t, carry):
        med_ref[:, tile(t)] = sum_tile(w, h, t)
        return carry

    lax.fori_loop(0, cols // LANES, body, 0, unroll=True)
    for n, (o, c) in enumerate(others):
        dist_copy(ITERS - 1, n, o, c, rank).wait_send()
    if groups > 1:
        for i in range(ITERS):
            for k in range(chunks):
                part_copy(i, k).wait_send()
        final_copy(0).wait_recv()
        total = total + last_in[:, pl.ds(0, LANES)]
    inverse = 1.0 / total

    def body(t, carry):
        m = med_ref[:, tile(t)]
        if groups > 1:
            m = m + last_in[:, after(t)]
        med_ref[:, tile(t)] = m * inverse
        return carry

    for k in range(len(ends) - 1):
        if groups > 1 and k > 0:
            final_copy(k).wait_recv()
        lax.fori_loop(ends[k], ends[k + 1], body, 0, unroll=True)
    for c in range(nc):
        share = (groups * clients) * weight[pl.ds(nc * j + c, 1), :] * inverse[0:1, :]
        share_ref[c] = share[0, 0]
    if groups > 1:
        for k in range(len(ends) - 1):
            final_copy(k).wait_send()


def local(updates, sample_counts):
    nc, rows, cols = updates.shape
    devices, cores = lax.axis_size("client"), lax.axis_size("param")
    groups = GROUPS if devices % GROUPS == 0 and devices > GROUPS else 1
    members = devices // groups
    tiles = cols // LANES
    bounds = sorted({0, tiles} | {round(end * tiles) for end in CHUNK_ENDS})
    ends = sorted({0, tiles} | {round(end * tiles) for end in LAST_ENDS})
    chunks = len(bounds) - 1
    mine = rows // devices
    if rows % devices or mine != SUBLANES or cols % LANES or members < 2 or members & (members - 1) or nc * members > LANES:
        return local_plain(updates, sample_counts)
    clients = nc * members
    f32 = jnp.float32
    dma = pltpu.SemaphoreType.DMA
    wide = cols + LANES
    return pl.pallas_call(
        functools.partial(kernel, groups, members, cores, bounds, ends),
        out_shape=(pltpu.VMEM((mine, cols), f32), pltpu.SMEM((nc,), f32)),
        in_specs=[pl.BlockSpec(memory_space=pltpu.HBM)] * 2,
        out_specs=(pl.BlockSpec(memory_space=pltpu.VMEM), pl.BlockSpec(memory_space=pltpu.SMEM)),
        scratch_shapes=[
            pltpu.VMEM((members, nc, groups, mine, cols), f32),
            pltpu.SMEM((nc,), jnp.int32),
            pltpu.VMEM((nc, LANES), f32),
            pltpu.VMEM((members, nc, LANES), f32),
            pltpu.VMEM((ITERS, 1, LANES), f32),
            pltpu.VMEM((ITERS, cores * members, 1, LANES), f32),
            pltpu.VMEM((clients, LANES), f32),
            pltpu.VMEM((clients, LANES), f32),
            pltpu.VMEM((ITERS, groups, mine, wide), f32),
            pltpu.VMEM((ITERS, groups, mine, wide), f32),
            pltpu.VMEM((mine, wide), f32),
            pltpu.VMEM((mine, wide), f32),
            dma,
            dma((chunks,)),
            dma((members, chunks)),
            dma((members, chunks)),
            dma((members,)),
            dma((members,)),
            dma((ITERS, chunks)),
            dma((ITERS, chunks)),
            dma((len(ends) - 1,)),
            dma((len(ends) - 1,)),
            dma((ITERS, cores * members)),
            dma((ITERS, cores * members)),
        ],
        compiler_params=pltpu.CompilerParams(
            collective_id=0, has_side_effects=True, vmem_limit_bytes=56 * 1024 * 1024),
        cost_estimate=pl.CostEstimate(
            flops=16 * clients * groups * mine * cols, bytes_accessed=8 * nc * rows * cols, transcendentals=0),
    )(updates.reshape(nc, groups, members, mine, cols), sample_counts)


def solution(mesh):
    return jax.shard_map(
        local,
        mesh=mesh,
        in_specs=(P("client", None, "param"), P("client")),
        out_specs=(P("client", "param"), P("client")),
        check_vma=False,
    )
```

```python
import functools

import jax
import jax.numpy as jnp
from jax import lax
from jax.experimental import pallas as pl
from jax.experimental.pallas import tpu as pltpu
from jax.sharding import PartitionSpec as P

ITERS = 2
LANES = 128
SUBLANES = 8
GROUPS = 1
CHUNK_ENDS = (0.5, 0.86, 1.0)
LAST_ENDS = (0.43, 1.0)

smoothing = 1e-06


def weighted_sum(weights, updates):
    return jnp.einsum("c,crk->rk", weights, updates, precision=lax.Precision.HIGHEST)


def local_plain(updates, sample_counts):
    local_clients = updates.shape[0]
    clients = local_clients * lax.axis_size("client")
    exchanged = lax.all_to_all(updates, "client", split_axis=1, concat_axis=0, tiled=True)
    counts_f = lax.all_gather(sample_counts, "client", axis=0, tiled=True).astype(jnp.float32)
    weights = counts_f
    for iteration in range(ITERS + 1):
        weight_sum = jnp.sum(weights)
        median = weighted_sum(weights, exchanged) / weight_sum
        if iteration < ITERS:
            distance_sq = jnp.sum((exchanged - median[None]) ** 2, axis=(1, 2))
            distance_sq = lax.psum(distance_sq, ("client", "param"))
            weights = counts_f / jnp.sqrt(distance_sq + smoothing)
    offset = lax.axis_index("client") * local_clients
    shares = lax.dynamic_slice_in_dim(clients * weights / weight_sum, offset, local_clients, 0)
    return (median, shares)


def kernel(groups, members, cores, bounds, ends, u_ref, cnt_hbm, med_ref, share_ref,
           held, cnt_ref, cnt_send, cnt_held, dist_send, dist_held, dist_rows, weight, part, part_in, last, last_in,
           in_sem, own_sem, u_send, u_recv, c_send, c_recv, p_send, p_recv, l_send, l_recv, d_send, d_recv):
    nc, cols = u_ref.shape[0], u_ref.shape[-1]
    clients = nc * members
    me, core = lax.axis_index("client"), lax.axis_index("param")
    j, h = lax.rem(me, members), lax.div(me, members)
    partner = lax.rem(me + members, groups * members)
    rank = core * members + j
    chunks = len(bounds) - 1

    def lanes(k):
        return pl.ds(bounds[k] * LANES, (bounds[k + 1] - bounds[k]) * LANES)

    def member(o, c):
        return {"client": h * members + flipped(o), "param": lax.rem(core + c, cores)}

    def flipped(m):
        return sum(b * lax.rem(lax.rem(lax.div(j, b), 2) + (m // b) % 2, 2) for b in bits)

    full = members - 1
    bits = [1 << b for b in range(full.bit_length())]
    others = sorted(((o, c) for c in range(cores) for o in range(members) if o or c),
                    key=lambda x: -bin(x[0]).count("1"))
    barrier = pltpu.get_barrier_semaphore()
    for o, c in others:
        pl.semaphore_signal(barrier, inc=1, device_id=member(o, c), device_id_type=pl.DeviceIdType.MESH)
    if groups > 1:
        pl.semaphore_signal(barrier, inc=1, device_id={"client": partner}, device_id_type=pl.DeviceIdType.MESH)
    counts_in = pltpu.make_async_copy(cnt_hbm, cnt_ref, in_sem)
    counts_in.start()
    own = []
    for k in range(chunks):
        sl = lanes(k)
        own.append(pltpu.make_async_copy(u_ref.at[:, :, j, :, sl], held.at[j, :, :, :, sl], own_sem.at[k]))
        own[-1].start()
    pl.semaphore_wait(barrier, len(others) + (groups > 1))

    masks = [full] + [m for low in range(members // 2 - 1, 0, -1) for m in (full - low, low)]

    def peer(o):
        m, index = masks[o - 1], 0
        for b in bits:
            flip = (m // b) % 2
            if m != full:
                flip = flip + lax.rem(core, 2) * (1 - 2 * flip)
            index = index + b * lax.rem(lax.rem(lax.div(j, b), 2) + flip, 2)
        return index

    def count_copy(o, slot):
        return pltpu.make_async_remote_copy(
            src_ref=cnt_send, dst_ref=cnt_held.at[slot], send_sem=c_send.at[o], recv_sem=c_recv.at[o],
            device_id={"client": h * members + peer(o)}, device_id_type=pl.DeviceIdType.MESH)

    def rows_copy(o, k, slot):
        to = peer(o)
        sl = lanes(k)
        return pltpu.make_async_remote_copy(
            src_ref=u_ref.at[:, :, to, :, sl], dst_ref=held.at[slot, :, :, :, sl],
            send_sem=u_send.at[o, k], recv_sem=u_recv.at[o, k],
            device_id={"client": h * members + to}, device_id_type=pl.DeviceIdType.MESH)

    for k in range(chunks):
        for o in range(1, members):
            rows_copy(o, k, j).start()
        if k == 0:
            counts_in.wait()
            for c in range(nc):
                row = jnp.full((1, LANES), cnt_ref[c], jnp.int32).astype(jnp.float32)
                cnt_send[c:c + 1, :] = row
                cnt_held[j, c:c + 1, :] = row
            for o in range(1, members):
                count_copy(o, j).start()

    def part_copy(i, k):
        first = bounds[k] + (k > 0)
        sl = pl.ds(first * LANES, (bounds[k + 1] + 1 - first) * LANES)
        return pltpu.make_async_remote_copy(
            src_ref=part.at[i, :, :, sl], dst_ref=part_in.at[i, :, :, sl],
            send_sem=p_send.at[i, k], recv_sem=p_recv.at[i, k],
            device_id={"client": partner}, device_id_type=pl.DeviceIdType.MESH)

    def dist_copy(i, n, o, c, slot):
        return pltpu.make_async_remote_copy(
            src_ref=dist_send.at[i], dst_ref=dist_held.at[i, slot],
            send_sem=d_send.at[i, n], recv_sem=d_recv.at[i, n],
            device_id=member(o, c), device_id_type=pl.DeviceIdType.MESH)

    def weights_now():
        w = [jnp.broadcast_to(weight[c:c + 1, :], (SUBLANES, LANES)) for c in range(clients)]
        total = w[0]
        for x in w[1:]:
            total = total + x
        return w, total

    def tile(t):
        return pl.ds(pl.multiple_of(t * LANES, LANES), LANES)

    def after(t):
        return pl.ds(pl.multiple_of((t + 1) * LANES, LANES), LANES)

    def sum_tile(w, r, t):
        sums = []
        for c in range(clients):
            x = w[c] * held[c // nc, c % nc, r, :, tile(t)]
            if c < 4:
                sums.append(x)
            else:
                sums[c % 4] = sums[c % 4] + x
        while len(sums) > 1:
            sums = [sums[n] + sums[n + 1] if n + 1 < len(sums) else sums[n] for n in range(0, len(sums), 2)]
        return sums[0]

    def iteration(i):
        w, total = weights_now()
        for r in range(groups):
            part[i, r, :, pl.ds(0, LANES)] = total

        def send_part(k):
            def body(t, carry):
                for r in range(groups):
                    part[i, r, :, after(t)] = sum_tile(w, r, t)
                return carry

            lax.fori_loop(bounds[k], bounds[k + 1], body, 0)
            if groups > 1:
                part_copy(i, k).start()

        def add_distances(k, inverse, acc):
            if groups > 1:
                part_copy(i, k).wait_recv()
            if inverse is None:
                whole = part[i, 0, :, pl.ds(0, LANES)]
                if groups > 1:
                    whole = whole + part_in[i, 0, :, pl.ds(0, LANES)]
                inverse = 1.0 / whole

            def body(t, acc):
                acc = list(acc)
                for r in range(groups):
                    m = part[i, r, :, after(t)]
                    if groups > 1:
                        m = m + part_in[i, r, :, after(t)]
                    m = m * inverse
                    for c in range(clients):
                        d = held[c // nc, c % nc, r, :, tile(t)] - m
                        acc[c] = acc[c] + d * d
                return tuple(acc)

            return inverse, lax.fori_loop(bounds[k], bounds[k + 1], body, acc)

        inverse, acc = None, tuple(jnp.zeros((SUBLANES, LANES), jnp.float32) for _ in range(clients))
        for k in range(chunks):
            if i == 0:
                own[k].wait()
                for o in range(1, members):
                    rows_copy(o, k, peer(o)).wait_recv()
            send_part(k)
            if i == 0 and k > 0:
                inverse, acc = add_distances(k - 1, inverse, acc)
        if i == 1:
            for o in range(1, members):
                count_copy(o, j).wait_send()
                for k in range(chunks):
                    rows_copy(o, k, j).wait_send()
        if i > 0:
            for n, (o, c) in enumerate(others):
                dist_copy(i - 1, n, o, c, rank).wait_send()
        for k in range(chunks - 1 if i == 0 else 0, chunks):
            inverse, acc = add_distances(k, inverse, acc)
        for c in range(clients):
            dist_rows[c:c + 1, :] = jnp.sum(acc[c], axis=0, keepdims=True)
        eye = (lax.broadcasted_iota(jnp.int32, (clients, LANES), 0)
               == lax.broadcasted_iota(jnp.int32, (clients, LANES), 1))
        column = jnp.sum(dist_rows[...], axis=1, keepdims=True)
        row = jnp.sum(jnp.where(eye, column, 0.0), axis=0, keepdims=True)
        dist_send[i] = row
        dist_held[i, rank] = row

        for n, (o, c) in enumerate(others):
            dist_copy(i, n, o, c, rank).start()
        for n, (o, c) in enumerate(others):
            dist_copy(i, n, o, c, lax.rem(core + cores - c, cores) * members + flipped(o)).wait_recv()
        row = dist_held[i, 0]
        for s in range(1, cores * members):
            row = row + dist_held[i, s]
        column = jnp.sum(jnp.where(eye, jnp.broadcast_to(row, eye.shape), 0.0), axis=1, keepdims=True)
        root = jnp.sqrt(jnp.broadcast_to(column, eye.shape) + smoothing)
        for c in range(clients):
            weight[c:c + 1, :] = cnt_held[c // nc, c % nc:c % nc + 1, :] / root[c:c + 1, :]

    for o in range(1, members):
        count_copy(o, peer(o)).wait_recv()
    for c in range(clients):
        weight[c:c + 1, :] = cnt_held[c // nc, c % nc:c % nc + 1, :]
    for i in range(ITERS):
        iteration(i)

    w, total = weights_now()
    def final_copy(k):
        first = ends[k] + (k > 0)
        sl = pl.ds(first * LANES, (ends[k + 1] + 1 - first) * LANES)
        return pltpu.make_async_remote_copy(
            src_ref=last.at[:, sl], dst_ref=last_in.at[:, sl], send_sem=l_send.at[k], recv_sem=l_recv.at[k],
            device_id={"client": partner}, device_id_type=pl.DeviceIdType.MESH)

    if groups > 1:
        last[:, pl.ds(0, LANES)] = total

        def body(t, carry):
            last[:, after(t)] = sum_tile(w, 1 - h, t)
            return carry

        for k in range(len(ends) - 1):
            lax.fori_loop(ends[k], ends[k + 1], body, 0)
            final_copy(k).start()

    def body(t, carry):
        med_ref[:, tile(t)] = sum_tile(w, h, t)
        return carry

    lax.fori_loop(0, cols // LANES, body, 0)
    for n, (o, c) in enumerate(others):
        dist_copy(ITERS - 1, n, o, c, rank).wait_send()
    if groups > 1:
        for i in range(ITERS):
            for k in range(chunks):
                part_copy(i, k).wait_send()
        final_copy(0).wait_recv()
        total = total + last_in[:, pl.ds(0, LANES)]
    inverse = 1.0 / total

    def body(t, carry):
        m = med_ref[:, tile(t)]
        if groups > 1:
            m = m + last_in[:, after(t)]
        med_ref[:, tile(t)] = m * inverse
        return carry

    for k in range(len(ends) - 1):
        if groups > 1 and k > 0:
            final_copy(k).wait_recv()
        lax.fori_loop(ends[k], ends[k + 1], body, 0)
    for c in range(nc):
        share = (groups * clients) * weight[pl.ds(nc * j + c, 1), :] * inverse[0:1, :]
        share_ref[c] = share[0, 0]
    if groups > 1:
        for k in range(len(ends) - 1):
            final_copy(k).wait_send()


def local(updates, sample_counts):
    nc, rows, cols = updates.shape
    devices, cores = lax.axis_size("client"), lax.axis_size("param")
    groups = GROUPS if devices % GROUPS == 0 and devices > GROUPS else 1
    members = devices // groups
    tiles = cols // LANES
    bounds = sorted({0, tiles} | {round(end * tiles) for end in CHUNK_ENDS})
    ends = sorted({0, tiles} | {round(end * tiles) for end in LAST_ENDS})
    chunks = len(bounds) - 1
    mine = rows // devices
    if rows % devices or mine != SUBLANES or cols % LANES or members < 2 or members & (members - 1) or nc * members > LANES:
        return local_plain(updates, sample_counts)
    clients = nc * members
    f32 = jnp.float32
    dma = pltpu.SemaphoreType.DMA
    wide = cols + LANES
    return pl.pallas_call(
        functools.partial(kernel, groups, members, cores, bounds, ends),
        out_shape=(pltpu.VMEM((mine, cols), f32), pltpu.SMEM((nc,), f32)),
        in_specs=[pl.BlockSpec(memory_space=pltpu.HBM)] * 2,
        out_specs=(pl.BlockSpec(memory_space=pltpu.VMEM), pl.BlockSpec(memory_space=pltpu.SMEM)),
        scratch_shapes=[
            pltpu.VMEM((members, nc, groups, mine, cols), f32),
            pltpu.SMEM((nc,), jnp.int32),
            pltpu.VMEM((nc, LANES), f32),
            pltpu.VMEM((members, nc, LANES), f32),
            pltpu.VMEM((ITERS, 1, LANES), f32),
            pltpu.VMEM((ITERS, cores * members, 1, LANES), f32),
            pltpu.VMEM((clients, LANES), f32),
            pltpu.VMEM((clients, LANES), f32),
            pltpu.VMEM((ITERS, groups, mine, wide), f32),
            pltpu.VMEM((ITERS, groups, mine, wide), f32),
            pltpu.VMEM((mine, wide), f32),
            pltpu.VMEM((mine, wide), f32),
            dma,
            dma((chunks,)),
            dma((members, chunks)),
            dma((members, chunks)),
            dma((members,)),
            dma((members,)),
            dma((ITERS, chunks)),
            dma((ITERS, chunks)),
            dma((len(ends) - 1,)),
            dma((len(ends) - 1,)),
            dma((ITERS, cores * members)),
            dma((ITERS, cores * members)),
        ],
        compiler_params=pltpu.CompilerParams(
            collective_id=0, has_side_effects=True, vmem_limit_bytes=56 * 1024 * 1024),
        cost_estimate=pl.CostEstimate(
            flops=16 * clients * groups * mine * cols, bytes_accessed=8 * nc * rows * cols, transcendentals=0),
    )(updates.reshape(nc, groups, members, mine, cols), sample_counts)


def solution(mesh):
    return jax.shard_map(
        local,
        mesh=mesh,
        in_specs=(P("client", None, "param"), P("client")),
        out_specs=(P("client", "param"), P("client")),
        check_vma=False,
    )
```
